512 devices in a mesh: dp: 8 (over x, core), proto: 64 (over z, y).
Axes of the slice: x: 4, y: 8, z: 8, core: 2. Of those that a mesh axis runs over, the one named last changes fastest.
Arguments:
- embeddings: bfloat16 [1024, 512], P('dp'), may hold values from -0.25 to 0.25
- prototypes: bfloat16 [131072, 512], P('proto'), may hold values from -0.25 to 0.25
- embedding_log_potential: float32 [1024], P('dp'), may hold values from -1.5 to 1.5
- prototype_log_potential: float32 [131072], P('proto'), may hold values from -1.5 to 1.5
- scaled_plan_gradient: bfloat16 [1024, 131072], P('dp', 'proto'), may hold values from -14 to 14
Outputs:
- grad_emb: float32 [1024, 512], P('dp', 'proto')
- grad_proto: bfloat16 [131072, 512], P('proto', 'dp')
The draws below stay inside these ranges and needn't reach their ends.
All inputs are finite; a program needn't handle non-finite values.
Results may differ from the reference program's by a relative error of at most 0.03.
Values may be sent and summed in bfloat16 or wider, within the bound.
A program may use at most 64 MiB of HBM per device.

```python
import math
import jax
import jax.numpy as jnp
from jax import lax

D = 512
TOK_DEV = 128
ITERS = 3
TOKENS = 1024
PROTOS = 131072
N_DP = 8


def shift_draw(key, count):
    position = jnp.arange(count).astype(jnp.float32) / count
    noise = jax.random.uniform(key, (count,), jnp.float32, -0.6, 0.6)
    return 1.1 * (position - 0.5) + noise


def draw_embedding_log_potential(key, part):
    key = jax.random.fold_in(key, 1)
    return shift_draw(key, TOKENS)


def draw_prototype_log_potential(key, part):
    key = jax.random.fold_in(key, 2)
    return shift_draw(key, PROTOS)


def draw_scaled_plan_gradient(key, part):
    key = jax.random.fold_in(key, 3)
    key_rows, key_cols, key_noise = jax.random.split(key, 3)
    rows = jax.random.truncated_normal(key_rows, -4.0, 4.0, (TOKENS, 1), jnp.float32)
    cols = jax.random.truncated_normal(key_cols, -4.0, 4.0, (1, PROTOS), jnp.float32)
    noise = jax.random.truncated_normal(key_noise, -4.0, 4.0, (TOKENS, PROTOS), jnp.float32)
    return (rows + cols + noise).astype(jnp.bfloat16)


def levels(own_key, dims, cuts, smallest, high):
    gain = 1.0
    for dim, blocks in cuts:
        draws = jax.random.uniform(jax.random.fold_in(jax.random.fold_in(own_key, 6), dim), (blocks,), jnp.float32, smallest / len(cuts), high / len(cuts))
        gain = gain * jnp.repeat(jnp.exp(draws), dims[dim] // blocks).reshape((-1,) + (1,) * (len(dims) - 1 - dim))
    return gain


def normal_values(own_key, shape, deviation, bound, cuts=(), kind=jnp.bfloat16):
    result = deviation * jax.random.normal(own_key, shape, jnp.float32)
    if cuts:
        result = result * levels(own_key, shape, cuts, -0.22, 0.18)
    return jnp.clip(result, -bound, bound).astype(kind)


def setup_inputs(seed: int = 0) -> dict:
    arg_keys = jax.random.split(jax.random.key(seed), 6)
    return {
        "embeddings": normal_values(arg_keys[0], (TOKENS, D), D ** -0.5, 0.25, ((0, 8),)),
        "prototypes": normal_values(arg_keys[1], (PROTOS, D), D ** -0.5, 0.25, ((0, 64),)),
        "embedding_log_potential": draw_embedding_log_potential(jax.random.fold_in(arg_keys[5], 71), 0),
        "prototype_log_potential": draw_prototype_log_potential(jax.random.fold_in(arg_keys[5], 71), 0),
        "scaled_plan_gradient": draw_scaled_plan_gradient(jax.random.fold_in(arg_keys[5], 71), 0),
    }


ENTROPY_TEMP_SCALE = 0.05
RIDGE_TERM = 0.05
HIGHEST_PREC = lax.Precision.HIGHEST

def reference(embeddings, prototypes, embedding_log_potential, prototype_log_potential, scaled_plan_gradient):
    n_total = embeddings.shape[0]
    k_total = prototypes.shape[0]
    width = embeddings.shape[1]
    root_rows = math.sqrt(n_total)
    root_cols = math.sqrt(k_total)
    similarity_scores = jnp.dot(embeddings, prototypes.T, preferred_element_type=jnp.float32)
    gibbs_kernel_matrix = jnp.exp(similarity_scores / ENTROPY_TEMP_SCALE + embedding_log_potential[:, None] + prototype_log_potential[None, :])
    weighted = scaled_plan_gradient.astype(jnp.float32) * gibbs_kernel_matrix
    row_marg = lax.optimization_barrier(jnp.sum(gibbs_kernel_matrix, axis=1)) / k_total + RIDGE_TERM
    col_marg = lax.optimization_barrier(jnp.sum(gibbs_kernel_matrix, axis=0)) / n_total + RIDGE_TERM
    rhs_rows = lax.optimization_barrier(jnp.sum(weighted, axis=1)) / root_cols
    rhs_cols = lax.optimization_barrier(jnp.sum(weighted, axis=0)) / root_rows
    coupling = 1.0 / (root_rows * root_cols)

    def apply_op(dir_rows, dir_cols):
        out_rows = row_marg * dir_rows + coupling * jnp.dot(gibbs_kernel_matrix, dir_cols, precision=HIGHEST_PREC)
        out_cols = col_marg * dir_cols + coupling * jnp.dot(dir_rows, gibbs_kernel_matrix, precision=HIGHEST_PREC)
        return (out_rows, out_cols)

    def inner(former, latter):
        return jnp.sum(former[0] * latter[0]) + jnp.sum(former[1] * latter[1])
    sol_rows = jnp.zeros_like(rhs_rows)
    sol_cols = jnp.zeros_like(rhs_cols)
    residual = (rhs_rows, rhs_cols)
    direction = (rhs_rows, rhs_cols)
    res_norm = inner(residual, residual)
    for iteration in range(ITERS):
        image = apply_op(direction[0], direction[1])
        step_size = res_norm / inner(direction, image)
        sol_rows = sol_rows + step_size * direction[0]
        sol_cols = sol_cols + step_size * direction[1]
        residual = (residual[0] - step_size * image[0], residual[1] - step_size * image[1])
        new_norm = inner(residual, residual)
        factor = new_norm / res_norm
        direction = (residual[0] + factor * direction[0], residual[1] + factor * direction[1])
        res_norm = new_norm
    implicit_adjustment = sol_rows[:, None] / root_cols + sol_cols[None, :] / root_rows
    prototype_weight = (gibbs_kernel_matrix * (scaled_plan_gradient.astype(jnp.float32) - implicit_adjustment) / ENTROPY_TEMP_SCALE).astype(jnp.bfloat16)
    grad_emb = jnp.dot(prototype_weight, prototypes, preferred_element_type=jnp.float32)
    weight_blocks = prototype_weight.reshape(N_DP, TOK_DEV, k_total)
    emb_blocks = embeddings.reshape(N_DP, TOK_DEV, width)

    def add_block(total, pair):
        block_weight, block_emb = pair
        partial_value = jnp.dot(block_weight.T, block_emb, preferred_element_type=jnp.float32).astype(jnp.bfloat16)
        partial_value = lax.optimization_barrier(partial_value)
        return (total + partial_value.astype(jnp.float32), None)
    grad_proto, unused = lax.scan(add_block, jnp.zeros((k_total, width), jnp.float32), (weight_blocks, emb_blocks))
    return (grad_emb, grad_proto.astype(jnp.bfloat16))
```

```python
import functools
import math

import jax
import jax.numpy as jnp
from jax import lax
from jax.experimental import pallas as pl
from jax.experimental.pallas import tpu as pltpu
from jax.sharding import PartitionSpec as P

MESH = pl.DeviceIdType.MESH
TEMP = 0.05
RIDGE = 0.05
N_DP = 8
N_Z = 8
N_Y = 8
N_PROTO = N_Z * N_Y
LANES = 128
F32 = jnp.float32
BF16 = jnp.bfloat16


def total(values):
    return jnp.sum(values, axis=1, keepdims=True)


def as_column(row):
    return jnp.broadcast_to(row, (LANES, LANES)).T


def as_row(acc):
    return jnp.sum(acc.T, axis=0, keepdims=True)


def far_first(i):
    return 4 + (1 - 2 * lax.rem(i, 2)) * lax.div(i + 1, 2)


def wait_bytes(ref, sem):
    pltpu.make_async_copy(ref, ref, sem).wait()


def solve(m0, b1, b2, r1r1, r1w, ww, waw):
    g00, g01, g02 = m0, b1 - r1r1, b2 - r1w
    g11, g12, g22 = r1w + r1r1, ww + r1w, waw
    l10, l20 = g01 / g00, g02 / g00
    d1 = g11 - g01 * l10
    i1 = jnp.where(d1 > 1e-6 * g11, 1.0 / d1, 0.0)
    t = g12 - l20 * g01
    l21 = t * i1
    d2 = g22 - l20 * g02 - l21 * t
    i2 = jnp.where(d2 > 1e-6 * g22, 1.0 / d2, 0.0)
    z1 = b1 - l10 * m0
    z2 = b2 - l20 * m0 - l21 * z1
    y2 = z2 * i2
    y1 = z1 * i1 - l21 * y2
    y0 = 1.0 - l10 * y1 - l20 * y2
    return y0, y1, y2


def body(
    rows_all, cols_all,
    e_hbm, p_hbm, er_hbm, pc_hbm, g_hbm, o_emb, o_proto,
    ev, et, pv, er, pc, gv, kv, wv, td1, td2, td3, tp1, tp2, rs_out, rs_in, gp_out, gp_in,
    in_sem, ready, send, recv,
):
    dp, pr = lax.axis_index("dp"), lax.axis_index("proto")
    z, y = lax.div(pr, N_Y), lax.rem(pr, N_Y)
    cols = pv.shape[0]
    tiles = cols // LANES
    root_cols = math.sqrt(cols_all)
    root_rows = math.sqrt(rows_all)
    coupling = 1.0 / (root_rows * root_cols)

    loads = [
        pltpu.make_async_copy(src, dst, in_sem.at[i])
        for i, (src, dst) in enumerate(
            [(e_hbm, ev), (p_hbm, pv), (er_hbm, er), (pc_hbm, pc), (g_hbm, gv)]
        )
    ]
    for load in loads:
        load.start()

    barrier = pltpu.get_barrier_semaphore()
    for k in range(1, 8):
        pl.semaphore_signal(
            barrier, inc=1, device_id=(lax.rem(dp + k, N_DP), pr), device_id_type=MESH
        )
        pl.semaphore_signal(
            barrier, inc=1, device_id=(dp, z * N_Y + lax.rem(y + k, N_Y)), device_id_type=MESH
        )
        pl.semaphore_signal(
            barrier, inc=1, device_id=(dp, lax.rem(z + k, N_Z) * N_Y + y), device_id_type=MESH
        )
    for load in loads:
        load.wait()

    def to_dp(buf, i):
        for k in range(1, N_DP):
            pltpu.make_async_remote_copy(
                src_ref=buf.at[dp], dst_ref=buf.at[dp], send_sem=send.at[i], recv_sem=recv.at[i],
                device_id=(lax.rem(dp + k, N_DP), pr), device_id_type=MESH,
            ).start()

    def to_proto(make, i):
        @pl.loop(0, N_PROTO - 1)
        def _(t):
            dz, dy = far_first(lax.div(t, N_Y)), far_first(lax.rem(t, N_Y))
            other = lax.rem(z + dz, N_Z) * N_Y + lax.rem(y + dy, N_Y)
            src, dst = make(other)
            pltpu.make_async_remote_copy(
                src_ref=src, dst_ref=dst, send_sem=send.at[i], recv_sem=recv.at[i],
                device_id=(dp, other), device_id_type=MESH,
            ).start()

    er_col = as_column(er[...])
    row_acc = jnp.zeros((LANES, LANES), F32)
    rhs_acc = jnp.zeros((LANES, LANES), F32)
    wide = 256
    er_wide = jnp.concatenate([er_col, er_col], axis=1)
    for c in range(cols // wide):
        at = pl.ds(c * wide, wide)
        scores = lax.dot_general(
            ev[...], pv[at, :], (((1,), (1,)), ((), ())), preferred_element_type=F32
        )
        k = jnp.exp(scores * (1.0 / TEMP) + er_wide + pc[:, at])
        kv[:, at] = k
        w = gv[:, at].astype(F32) * k
        td1[dp, 0:1, at] = jnp.sum(k, axis=0, keepdims=True)
        td1[dp, 1:2, at] = jnp.sum(w, axis=0, keepdims=True)
        row_acc += k[:, :LANES] + k[:, LANES:]
        rhs_acc += w[:, :LANES] + w[:, LANES:]

    pl.semaphore_wait(barrier, 21)
    to_dp(td1, 0)
    for k in range(1, 8):
        pl.semaphore_signal(
            ready, inc=1, device_id=(dp, lax.rem(z + k, N_Z) * N_Y + y), device_id_type=MESH
        )
    row_part = as_row(row_acc)
    rhs_part = as_row(rhs_acc)
    et[...] = jnp.concatenate(
        [ev[:, j * LANES : (j + 1) * LANES].astype(F32).T for j in range(et.shape[0] // LANES)],
        axis=0,
    ).astype(BF16)
    wait_bytes(td1.at[pl.ds(0, N_DP - 1)], recv.at[0])
    col_pair = jnp.sum(td1[...], axis=0)
    dc = col_pair[0:1] * (1.0 / rows_all) + RIDGE
    v0c = col_pair[1:2] * (1.0 / root_rows)

    def lanes(row, t):
        return row[:, t * LANES : (t + 1) * LANES]

    def fold(row):
        return functools.reduce(lambda a, b: a + b, [lanes(row, t) for t in range(tiles)])

    def k_times(*vectors):
        accs = [jnp.zeros((LANES, LANES), F32) for _ in vectors]
        for t in range(tiles):
            k = kv[:, t * LANES : (t + 1) * LANES]
            accs = [a + k * lanes(v, t) for a, v in zip(accs, vectors)]
        return [as_row(a) for a in accs]

    (kv0,) = k_times(v0c)
    tp1[pr] = jnp.concatenate(
        [row_part, rhs_part, kv0, fold(v0c * v0c), fold(v0c * dc * v0c), jnp.zeros((3, LANES), F32)],
        axis=0,
    )
    pl.semaphore_wait(ready, 7)
    to_proto(lambda other: (tp1.at[pr], tp1.at[pr]), 1)
    wait_bytes(tp1.at[pl.ds(0, N_PROTO - 1)], recv.at[1])
    one = jnp.sum(tp1[...], axis=0)
    dr = one[0:1] * (1.0 / cols_all) + RIDGE
    v0r = one[1:2] * (1.0 / root_cols)
    kv0 = one[2:3]
    s0, s1 = total(one[3:4]), total(one[4:5])
    p_r = dr * v0r + coupling * kv0

    v0_col, p_col = as_column(v0r), as_column(p_r)
    for t in range(tiles):
        at = pl.ds(t * LANES, LANES)
        k = kv[:, at]
        td2[dp, 0:1, at] = jnp.sum(k * v0_col, axis=0, keepdims=True)
        td2[dp, 1:2, at] = jnp.sum(k * p_col, axis=0, keepdims=True)
    td2[dp, 0:1, pl.ds(cols, LANES)] = v0r * v0r
    td2[dp, 1:2, pl.ds(cols, LANES)] = v0r * (dr * v0r + (2.0 * coupling) * kv0)
    to_dp(td2, 2)
    wait_bytes(td2.at[pl.ds(0, N_DP - 1)], recv.at[2])
    two = jnp.sum(td2[...], axis=0)
    m0 = s0 + total(two[0:1, cols:])
    m1 = s1 + total(two[1:2, cols:])
    theta = m1 / m0
    step = m0 / m1
    ktv0, ktp = two[0:1, :cols], two[1:2, :cols]
    r1r = v0r - step * p_r
    r1c = v0c - step * (dc * v0c + coupling * ktv0)
    ktr1 = ktv0 - step * ktp
    wc = step * (dc * r1c + coupling * ktr1) - r1c

    kr1, kw = k_times(r1c, wc)
    tp2[pr] = jnp.concatenate(
        [kr1, kw, fold(r1c * r1c), fold(r1c * wc), fold(v0c * wc), fold(wc * wc),
         fold(wc * dc * wc), fold(v0c * r1c)],
        axis=0,
    )
    to_proto(lambda other: (tp2.at[pr], tp2.at[pr]), 3)
    wait_bytes(tp2.at[pl.ds(0, N_PROTO - 1)], recv.at[3])
    three = jnp.sum(tp2[...], axis=0)
    kr1, kw = three[0:1], three[1:2]
    wr = step * (dr * r1r + coupling * kr1) - r1r
    td3[dp] = jnp.concatenate(
        [r1r * r1r, r1r * wr, v0r * wr, wr * wr, wr * (dr * wr + (2.0 * coupling) * kw), v0r * r1r,
         jnp.zeros((2, LANES), F32)],
        axis=0,
    )
    to_dp(td3, 4)
    wait_bytes(td3.at[pl.ds(0, N_DP - 1)], recv.at[4])
    four = total(jnp.sum(td3[...], axis=0))
    five = total(three)
    r1r1, r1w = four[0:1] + five[2:3], four[1:2] + five[3:4]
    v0w, ww = four[2:3] + five[4:5], four[3:4] + five[5:6]
    waw = (four[4:5] + five[6:7]) * step
    v0r1 = four[5:6] + five[7:8]
    y0, y1, y2 = solve(m0, v0r1, v0w, r1r1, r1w, ww, waw)
    y0, y1, y2 = y0 * step, y1 * step, y2 * step
    sol_r = (y0 * v0r + y1 * r1r + y2 * wr) * (1.0 / root_cols)
    sol_c = (y0 * v0c + y1 * r1c + y2 * wc) * (1.0 / root_rows)

    sol_col = as_column(sol_r)
    for t in range(tiles):
        at = pl.ds(t * LANES, LANES)
        g = gv[:, at].astype(F32)
        wv[:, at] = (kv[:, at] * (g - sol_col - lanes(sol_c, t)) * (1.0 / TEMP)).astype(BF16)
    ge = jnp.dot(wv[...], pv[...], preferred_element_type=F32)
    for j in range(4):
        rs_out[pl.ds(16 * j, 16)] = ge[:, j * LANES : (j + 1) * LANES].T.reshape(16, 8, LANES)
    to_proto(lambda other: (rs_out.at[other], rs_in.at[pr]), 5)
    rs_in[pr] = rs_out[pr]

    def proto_terms(d):
        part = et[pl.ds(pl.multiple_of(d * 64, 64), 64), :]
        gp_out[d] = jnp.dot(part, wv[...], preferred_element_type=F32).astype(BF16)

    for k in range(1, N_DP):
        d = lax.rem(dp + k, N_DP)
        proto_terms(d)
        pltpu.make_async_remote_copy(
            src_ref=gp_out.at[d], dst_ref=gp_in.at[dp], send_sem=send.at[6], recv_sem=recv.at[6],
            device_id=(d, pr), device_id_type=MESH,
        ).start()
    proto_terms(dp)
    gp_in[dp] = gp_out[dp]
    wait_bytes(rs_in.at[pl.ds(0, N_PROTO - 1)], recv.at[5])
    o_emb[...] = jnp.sum(rs_in[...], axis=0)
    wait_bytes(gp_in.at[pl.ds(0, N_DP - 1)], recv.at[6])
    for c in range(cols // 512):
        at = pl.ds(c * 512, 512)
        acc = gp_in[0, :, at].astype(F32)
        for d in range(1, N_DP):
            acc += gp_in[d, :, at].astype(F32)
        o_proto[:, at] = acc.astype(BF16)

    wait_bytes(td1.at[pl.ds(0, N_DP - 1)], send.at[0])
    wait_bytes(tp1.at[pl.ds(0, N_PROTO - 1)], send.at[1])
    wait_bytes(td2.at[pl.ds(0, N_DP - 1)], send.at[2])
    wait_bytes(tp2.at[pl.ds(0, N_PROTO - 1)], send.at[3])
    wait_bytes(td3.at[pl.ds(0, N_DP - 1)], send.at[4])
    wait_bytes(rs_out.at[pl.ds(0, N_PROTO - 1)], send.at[5])
    wait_bytes(gp_out.at[pl.ds(0, N_DP - 1)], send.at[6])


def shards(
    embeddings, prototypes, embedding_log_potential, prototype_log_potential, scaled_plan_gradient
):
    rows, width = embeddings.shape
    cols = prototypes.shape[0]
    share = width // N_DP
    any_space = pl.BlockSpec(memory_space=pl.ANY)
    vmem = pl.BlockSpec(memory_space=pltpu.VMEM)
    ge, gp = pl.pallas_call(
        functools.partial(body, rows * N_DP, cols * N_PROTO),
        out_shape=(
            jax.ShapeDtypeStruct((width // N_PROTO, rows), F32),
            jax.ShapeDtypeStruct((share, cols), BF16),
        ),
        in_specs=[any_space] * 5,
        out_specs=(vmem, vmem),
        scratch_shapes=[
            pltpu.VMEM((rows, width), BF16),
            pltpu.VMEM((width, rows), BF16),
            pltpu.VMEM((cols, width), BF16),
            pltpu.VMEM((1, rows), F32),
            pltpu.VMEM((1, cols), F32),
            pltpu.VMEM((rows, cols), BF16),
            pltpu.VMEM((rows, cols), F32),
            pltpu.VMEM((rows, cols), BF16),
            pltpu.VMEM((N_DP, 2, cols), F32),
            pltpu.VMEM((N_DP, 2, cols + LANES), F32),
            pltpu.VMEM((N_DP, 8, LANES), F32),
            pltpu.VMEM((N_PROTO, 8, LANES), F32),
            pltpu.VMEM((N_PROTO, 8, LANES), F32),
            pltpu.VMEM((N_PROTO, 8, LANES), F32),
            pltpu.VMEM((N_PROTO, 8, LANES), F32),
            pltpu.VMEM((N_DP, share, cols), BF16),
            pltpu.VMEM((N_DP, share, cols), BF16),
            pltpu.SemaphoreType.DMA((5,)),
            pltpu.SemaphoreType.REGULAR,
            pltpu.SemaphoreType.DMA((7,)),
            pltpu.SemaphoreType.DMA((7,)),
        ],
        compiler_params=pltpu.CompilerParams(
            collective_id=0, has_side_effects=True, vmem_limit_bytes=56 * 1024 * 1024
        ),
    )(
        embeddings,
        prototypes,
        embedding_log_potential.reshape(1, rows),
        prototype_log_potential.reshape(1, cols),
        scaled_plan_gradient,
    )
    return ge.T, gp.T


def solution(mesh):
    return jax.shard_map(
        shards,
        mesh=mesh,
        in_specs=(P("dp", None), P("proto", None), P("dp"), P("proto"), P("dp", "proto")),
        out_specs=(P("dp", "proto"), P("proto", "dp")),
        check_vma=False,
    )
```

```python
import functools
import math

import jax
import jax.numpy as jnp
from jax import lax
from jax.experimental import pallas as pl
from jax.experimental.pallas import tpu as pltpu
from jax.sharding import PartitionSpec as P

MESH = pl.DeviceIdType.MESH
TEMP = 0.05
EARLY = 3
RIDGE = 0.05
N_DP = 8
N_Z = 8
N_Y = 8
N_PROTO = N_Z * N_Y
LANES = 128
F32 = jnp.float32
BF16 = jnp.bfloat16


def total(values):
    return jnp.sum(values, axis=1, keepdims=True)


def as_column(row):
    return jnp.broadcast_to(row, (LANES, LANES)).T


def as_row(acc):
    return jnp.sum(acc.T, axis=0, keepdims=True)


def hops(dz, dy):
    return min(dz, N_Z - dz) + min(dy, N_Y - dy)


FAR_FIRST = sorted(
    [(dz, dy) for dz in range(N_Z) for dy in range(N_Y) if dz or dy], key=lambda o: -hops(*o)
)
DP_FAR_FIRST = (4, 5, 3, 2, 6, 1, 7)


def wait_bytes(ref, sem):
    pltpu.make_async_copy(ref, ref, sem).wait()


def solve(m0, b1, b2, r1r1, r1w, ww, waw):
    g00, g01, g02 = m0, b1 - r1r1, b2 - r1w
    g11, g12, g22 = r1w + r1r1, ww + r1w, waw
    l10, l20 = g01 / g00, g02 / g00
    d1 = g11 - g01 * l10
    i1 = jnp.where(d1 > 1e-6 * g11, 1.0 / d1, 0.0)
    t = g12 - l20 * g01
    l21 = t * i1
    d2 = g22 - l20 * g02 - l21 * t
    i2 = jnp.where(d2 > 1e-6 * g22, 1.0 / d2, 0.0)
    z1 = b1 - l10 * m0
    z2 = b2 - l20 * m0 - l21 * z1
    y2 = z2 * i2
    y1 = z1 * i1 - l21 * y2
    y0 = 1.0 - l10 * y1 - l20 * y2
    return y0, y1, y2


def body(
    rows_all, cols_all,
    e_hbm, p_hbm, er_hbm, pc_hbm, g_hbm, o_emb, o_proto,
    ev, et, pv, er, pc, gv, kv, wv, td1, td2, td3, tp1, tp2, rs_out, rs_in,
    ef, eg, erc, kf, uf, sf, sp_out, sp_own, sp_in, sx,
    in_sem, ready, send, recv,
):
    dp, pr = lax.axis_index("dp"), lax.axis_index("proto")
    z, y = lax.div(pr, N_Y), lax.rem(pr, N_Y)
    cols = pv.shape[0]
    tiles = cols // LANES
    root_cols = math.sqrt(cols_all)
    root_rows = math.sqrt(rows_all)
    coupling = 1.0 / (root_rows * root_cols)

    loads = [
        pltpu.make_async_copy(src, dst, in_sem.at[i])
        for i, (src, dst) in enumerate(
            [(e_hbm, ev), (p_hbm, pv), (er_hbm, er), (pc_hbm, pc), (g_hbm, gv)]
        )
    ]
    for load in loads:
        load.start()

    barrier = pltpu.get_barrier_semaphore()
    for k in range(1, 8):
        pl.semaphore_signal(
            barrier, inc=1, device_id=(lax.rem(dp + k, N_DP), pr), device_id_type=MESH
        )
        pl.semaphore_signal(
            barrier, inc=1, device_id=(dp, z * N_Y + lax.rem(y + k, N_Y)), device_id_type=MESH
        )
        pl.semaphore_signal(
            barrier, inc=1, device_id=(dp, lax.rem(z + k, N_Z) * N_Y + y), device_id_type=MESH
        )
    for load in loads:
        load.wait()

    def to_dp(buf, i):
        for k in DP_FAR_FIRST:
            pltpu.make_async_remote_copy(
                src_ref=buf.at[dp], dst_ref=buf.at[dp], send_sem=send.at[i], recv_sem=recv.at[i],
                device_id=(lax.rem(dp + k, N_DP), pr), device_id_type=MESH,
            ).start()

    def to_proto(make, i):
        for dz, dy in FAR_FIRST:
            other = lax.rem(z + dz, N_Z) * N_Y + lax.rem(y + dy, N_Y)
            src, dst = make(other)
            pltpu.make_async_remote_copy(
                src_ref=src, dst_ref=dst, send_sem=send.at[i], recv_sem=recv.at[i],
                device_id=(dp, other), device_id_type=MESH,
            ).start()

    er_col = as_column(er[...])
    row_acc = jnp.zeros((LANES, LANES), F32)
    rhs_acc = jnp.zeros((LANES, LANES), F32)
    wide = 256
    er_wide = jnp.concatenate([er_col, er_col], axis=1)
    for c in range(cols // wide):
        at = pl.ds(c * wide, wide)
        scores = lax.dot_general(
            ev[...], pv[at, :], (((1,), (1,)), ((), ())), preferred_element_type=F32
        )
        k = jnp.exp(scores * (1.0 / TEMP) + er_wide + pc[:, at])
        kv[:, at] = k
        w = gv[:, at].astype(F32) * k
        td1[dp, 0:1, at] = jnp.sum(k, axis=0, keepdims=True)
        td1[dp, 1:2, at] = jnp.sum(w, axis=0, keepdims=True)
        row_acc += k[:, :LANES] + k[:, LANES:]
        rhs_acc += w[:, :LANES] + w[:, LANES:]
        wv[:, at] = w.astype(BF16)
    td1[dp, 0:1, pl.ds(cols, LANES)] = er[...]
    td1[dp, 1:2, pl.ds(cols, LANES)] = er[...]
    mine = pl.ds(pl.multiple_of(dp * LANES, LANES), LANES)

    pl.semaphore_wait(barrier, 21)
    to_dp(td1, 0)
    for k in range(1, 8):
        pl.semaphore_signal(
            ready, inc=1, device_id=(dp, lax.rem(z + k, N_Z) * N_Y + y), device_id_type=MESH
        )
    row_part = as_row(row_acc)
    rhs_part = as_row(rhs_acc)

    for j in range(N_DP // 2):
        pair = ev[:, j * LANES : (j + 1) * LANES].astype(F32).T.astype(BF16)
        et[2 * j] = pair[:64]
        et[2 * j + 1] = pair[64:]
    for k in DP_FAR_FIRST:
        d = lax.rem(dp + k, N_DP)
        pltpu.make_async_remote_copy(
            src_ref=et.at[d], dst_ref=eg.at[dp], send_sem=send.at[7], recv_sem=recv.at[7],
            device_id=(d, pr), device_id_type=MESH,
        ).start()
        pltpu.make_async_remote_copy(
            src_ref=ev, dst_ref=ef.at[mine], send_sem=send.at[6], recv_sem=recv.at[6],
            device_id=(d, pr), device_id_type=MESH,
        ).start()
    eg[dp] = et[dp]
    ef[mine, :] = ev[...]

    def weighted_terms(to, first):
        lhs = jnp.concatenate([et[2 * j + first] for j in range(4)], axis=0)
        for c in range(cols // 512):
            at = pl.ds(c * 512, 512)
            part = jnp.dot(lhs, wv[:, at], preferred_element_type=F32).astype(BF16)
            for j in range(4):
                to[j, :, at] = part[64 * j : 64 * j + 64]

    x, core = lax.div(dp, 2), lax.rem(dp, 2)
    weighted_terms(sp_out, 1 - core)
    pltpu.make_async_remote_copy(
        src_ref=sp_out, dst_ref=sp_in, send_sem=send.at[8], recv_sem=recv.at[8],
        device_id=(2 * x + 1 - core, pr), device_id_type=MESH,
    ).start()
    weighted_terms(sp_own, core)
    wait_bytes(td1.at[pl.ds(0, N_DP - 1)], recv.at[0])
    col_pair = jnp.sum(td1[:, :, pl.ds(0, cols)], axis=0)
    dc = col_pair[0:1] * (1.0 / rows_all) + RIDGE
    v0c = col_pair[1:2] * (1.0 / root_rows)

    def lanes(row, t):
        return row[:, t * LANES : (t + 1) * LANES]

    def fold(row):
        return functools.reduce(lambda a, b: a + b, [lanes(row, t) for t in range(tiles)])

    def k_times(*vectors):
        accs = [jnp.zeros((LANES, LANES), F32) for _ in vectors]
        for t in range(tiles):
            k = kv[:, t * LANES : (t + 1) * LANES]
            accs = [a + k * lanes(v, t) for a, v in zip(accs, vectors)]
        return [as_row(a) for a in accs]

    (kv0,) = k_times(v0c)
    tp1[pr] = jnp.concatenate(
        [row_part, rhs_part, kv0, fold(v0c * v0c), fold(v0c * dc * v0c), jnp.zeros((3, LANES), F32)],
        axis=0,
    )
    pl.semaphore_wait(ready, 7)
    to_proto(lambda other: (tp1.at[pr], tp1.at[pr]), 1)

    wait_bytes(sp_in, recv.at[8])
    for k in (2, 1, 3):
        other = lax.rem(x + k, 4)
        sp_own[other] = (sp_own[other].astype(F32) + sp_in[other].astype(F32)).astype(BF16)
        pltpu.make_async_remote_copy(
            src_ref=sp_own.at[other], dst_ref=sx.at[x], send_sem=send.at[9], recv_sem=recv.at[9],
            device_id=(2 * other + core, pr), device_id_type=MESH,
        ).start()
    sx[x] = (sp_own[x].astype(F32) + sp_in[x].astype(F32)).astype(BF16)
    for d in range(N_DP):
        erc[d * LANES : (d + 1) * LANES, :] = as_column(td1[d, 0:1, cols:])
    wait_bytes(tp1.at[pl.ds(0, N_PROTO - 1)], recv.at[1])
    one = jnp.sum(tp1[...], axis=0)
    dr = one[0:1] * (1.0 / cols_all) + RIDGE
    v0r = one[1:2] * (1.0 / root_cols)
    kv0 = one[2:3]
    s0, s1 = total(one[3:4]), total(one[4:5])
    p_r = dr * v0r + coupling * kv0

    v0_col, p_col = as_column(v0r), as_column(p_r)
    for t in range(tiles):
        at = pl.ds(t * LANES, LANES)
        k = kv[:, at]
        td2[dp, 0:1, at] = jnp.sum(k * v0_col, axis=0, keepdims=True)
        td2[dp, 1:2, at] = jnp.sum(k * p_col, axis=0, keepdims=True)
    td2[dp, 0:1, pl.ds(cols, LANES)] = v0r * v0r
    td2[dp, 1:2, pl.ds(cols, LANES)] = v0r * (dr * v0r + (2.0 * coupling) * kv0)
    td2[dp, 0:1, pl.ds(cols + LANES, LANES)] = v0r
    td2[dp, 1:2, pl.ds(cols + LANES, LANES)] = p_r
    to_dp(td2, 2)

    def whole_kernel(c):
        at = pl.ds(c * wide, wide)
        scores = lax.dot_general(
            ef[...], pv[at, :], (((1,), (1,)), ((), ())), preferred_element_type=F32
        )
        shift = jnp.concatenate([erc[...], erc[...]], axis=1)
        kf[:, at] = jnp.exp(scores * (1.0 / TEMP) + shift + pc[:, at]).astype(BF16)

    wait_bytes(ef.at[pl.ds(0, (N_DP - 1) * LANES)], recv.at[6])
    wait_bytes(eg.at[pl.ds(0, N_DP - 1)], recv.at[7])
    for c in range(EARLY):
        whole_kernel(c)
    wait_bytes(td2.at[pl.ds(0, N_DP - 1)], recv.at[2])
    two = jnp.sum(td2[...], axis=0)
    m0 = s0 + total(two[0:1, cols : cols + LANES])
    m1 = s1 + total(two[1:2, cols : cols + LANES])
    theta = m1 / m0
    step = m0 / m1
    ktv0, ktp = two[0:1, :cols], two[1:2, :cols]
    r1r = v0r - step * p_r
    r1c = v0c - step * (dc * v0c + coupling * ktv0)
    ktr1 = ktv0 - step * ktp
    wc = step * (dc * r1c + coupling * ktr1) - r1c

    kr1, kw = k_times(r1c, wc)
    tp2[pr] = jnp.concatenate(
        [kr1, kw, fold(r1c * r1c), fold(r1c * wc), fold(v0c * wc), fold(wc * wc),
         fold(wc * dc * wc), fold(v0c * r1c)],
        axis=0,
    )
    to_proto(lambda other: (tp2.at[pr], tp2.at[pr]), 3)
    for c in range(EARLY, cols // wide):
        whole_kernel(c)
    lhs = jnp.concatenate([eg[d] for d in range(N_DP)], axis=1)
    for c in range(cols // 512):
        at = pl.ds(c * 512, 512)
        uf[:, at] = jnp.dot(lhs, kf[:, at], preferred_element_type=F32)
    wait_bytes(tp2.at[pl.ds(0, N_PROTO - 1)], recv.at[3])
    three = jnp.sum(tp2[...], axis=0)
    kr1, kw = three[0:1], three[1:2]
    wr = step * (dr * r1r + coupling * kr1) - r1r
    td3[dp] = jnp.concatenate(
        [r1r * r1r, r1r * wr, v0r * wr, wr * wr, wr * (dr * wr + (2.0 * coupling) * kw), v0r * r1r,
         wr, jnp.zeros((1, LANES), F32)],
        axis=0,
    )
    to_dp(td3, 4)
    wait_bytes(sx.at[pl.ds(0, 3)], recv.at[9])
    for c in range(cols // 512):
        at = pl.ds(c * 512, 512)
        acc = sx[0, :, at].astype(F32)
        for j in range(1, 4):
            acc += sx[j, :, at].astype(F32)
        sf[:, at] = acc
    wait_bytes(td3.at[pl.ds(0, N_DP - 1)], recv.at[4])
    four = total(jnp.sum(td3[...], axis=0))
    five = total(three)
    r1r1, r1w = four[0:1] + five[2:3], four[1:2] + five[3:4]
    v0w, ww = four[2:3] + five[4:5], four[3:4] + five[5:6]
    waw = (four[4:5] + five[6:7]) * step
    v0r1 = four[5:6] + five[7:8]
    y0, y1, y2 = solve(m0, v0r1, v0w, r1r1, r1w, ww, waw)
    y0, y1, y2 = y0 * step, y1 * step, y2 * step
    sol_r = (y0 * v0r + y1 * r1r + y2 * wr) * (1.0 / root_cols)
    sol_c = (y0 * v0c + y1 * r1c + y2 * wc) * (1.0 / root_rows)

    sol_col = as_column(sol_r)
    for t in range(tiles):
        at = pl.ds(t * LANES, LANES)
        g = gv[:, at].astype(F32)
        wv[:, at] = (kv[:, at] * (g - sol_col - lanes(sol_c, t)) * (1.0 / TEMP)).astype(BF16)
    ge = jnp.dot(wv[...], pv[...], preferred_element_type=F32)
    for j in range(4):
        rs_out[pl.ds(16 * j, 16)] = ge[:, j * LANES : (j + 1) * LANES].T.reshape(16, 8, LANES)
    to_proto(lambda other: (rs_out.at[other], rs_in.at[pr]), 5)
    rs_in[pr] = rs_out[pr]

    scaled = []
    for d in range(N_DP):
        v0d = td2[d, 0:1, pl.ds(cols + LANES, LANES)]
        r1d = v0d - step * td2[d, 1:2, pl.ds(cols + LANES, LANES)]
        sol_d = (y0 * v0d + y1 * r1d + y2 * td3[d, 6:7, :]) * (1.0 / root_cols)
        scaled.append((eg[d].astype(F32) * sol_d).astype(BF16))
    lhs = jnp.concatenate(scaled, axis=1)
    for c in range(cols // 512):
        at = pl.ds(c * 512, 512)
        terms = jnp.dot(lhs, kf[:, at], preferred_element_type=F32)
        part = sf[:, at] - terms - uf[:, at] * sol_c[:, c * 512 : (c + 1) * 512]
        o_proto[:, at] = (part * (1.0 / TEMP)).astype(BF16)
    wait_bytes(rs_in.at[pl.ds(0, N_PROTO - 1)], recv.at[5])
    o_emb[...] = jnp.sum(rs_in[...], axis=0)

    wait_bytes(td1.at[pl.ds(0, N_DP - 1)], send.at[0])
    wait_bytes(tp1.at[pl.ds(0, N_PROTO - 1)], send.at[1])
    wait_bytes(td2.at[pl.ds(0, N_DP - 1)], send.at[2])
    wait_bytes(tp2.at[pl.ds(0, N_PROTO - 1)], send.at[3])
    wait_bytes(td3.at[pl.ds(0, N_DP - 1)], send.at[4])
    wait_bytes(rs_out.at[pl.ds(0, N_PROTO - 1)], send.at[5])
    wait_bytes(ef.at[pl.ds(0, (N_DP - 1) * LANES)], send.at[6])
    wait_bytes(et.at[pl.ds(0, N_DP - 1)], send.at[7])
    wait_bytes(sp_out, send.at[8])
    wait_bytes(sp_own.at[pl.ds(0, 3)], send.at[9])


def shards(
    embeddings, prototypes, embedding_log_potential, prototype_log_potential, scaled_plan_gradient
):
    rows, width = embeddings.shape
    cols = prototypes.shape[0]
    share = width // N_DP
    any_space = pl.BlockSpec(memory_space=pl.ANY)
    vmem = pl.BlockSpec(memory_space=pltpu.VMEM)
    ge, gp = pl.pallas_call(
        functools.partial(body, rows * N_DP, cols * N_PROTO),
        out_shape=(
            jax.ShapeDtypeStruct((width // N_PROTO, rows), F32),
            jax.ShapeDtypeStruct((share, cols), BF16),
        ),
        in_specs=[any_space] * 5,
        out_specs=(vmem, vmem),
        scratch_shapes=[
            pltpu.VMEM((rows, width), BF16),
            pltpu.VMEM((N_DP, share, rows), BF16),
            pltpu.VMEM((cols, width), BF16),
            pltpu.VMEM((1, rows), F32),
            pltpu.VMEM((1, cols), F32),
            pltpu.VMEM((rows, cols), BF16),
            pltpu.VMEM((rows, cols), F32),
            pltpu.VMEM((rows, cols), BF16),
            pltpu.VMEM((N_DP, 2, cols + LANES), F32),
            pltpu.VMEM((N_DP, 2, cols + 2 * LANES), F32),
            pltpu.VMEM((N_DP, 8, LANES), F32),
            pltpu.VMEM((N_PROTO, 8, LANES), F32),
            pltpu.VMEM((N_PROTO, 8, LANES), F32),
            pltpu.VMEM((N_PROTO, 8, LANES), F32),
            pltpu.VMEM((N_PROTO, 8, LANES), F32),
            pltpu.VMEM((rows * N_DP, width), BF16),
            pltpu.VMEM((N_DP, share, rows), BF16),
            pltpu.VMEM((rows * N_DP, LANES), F32),
            pltpu.VMEM((rows * N_DP, cols), BF16),
            pltpu.VMEM((share, cols), F32),
            pltpu.VMEM((share, cols), F32),
            pltpu.VMEM((4, share, cols), BF16),
            pltpu.VMEM((4, share, cols), BF16),
            pltpu.VMEM((4, share, cols), BF16),
            pltpu.VMEM((4, share, cols), BF16),
            pltpu.SemaphoreType.DMA((5,)),
            pltpu.SemaphoreType.REGULAR,
            pltpu.SemaphoreType.DMA((10,)),
            pltpu.SemaphoreType.DMA((10,)),
        ],
        compiler_params=pltpu.CompilerParams(
            collective_id=0, has_side_effects=True, vmem_limit_bytes=56 * 1024 * 1024
        ),
    )(
        embeddings,
        prototypes,
        embedding_log_potential.reshape(1, rows),
        prototype_log_potential.reshape(1, cols),
        scaled_plan_gradient,
    )
    return ge.T, gp.T


def solution(mesh):
    return jax.shard_map(
        shards,
        mesh=mesh,
        in_specs=(P("dp", None), P("proto", None), P("dp"), P("proto"), P("dp", "proto")),
        out_specs=(P("dp", "proto"), P("proto", "dp")),
        check_vma=False,
    )
```

```python
import functools
import math

import jax
import jax.numpy as jnp
from jax import lax
from jax.experimental import pallas as pl
from jax.experimental.pallas import tpu as pltpu
from jax.sharding import PartitionSpec as P

MESH = pl.DeviceIdType.MESH
TEMP = 0.05
RIDGE = 0.05
N_DP = 8
N_Z = 8
N_Y = 8
N_PROTO = N_Z * N_Y
LANES = 128
F32 = jnp.float32
BF16 = jnp.bfloat16


def total(values):
    return jnp.sum(values, axis=1, keepdims=True)


def as_column(row):
    return jnp.broadcast_to(row, (LANES, LANES)).T


def as_row(acc):
    return jnp.sum(acc.T, axis=0, keepdims=True)


def hops(dz, dy):
    return min(dz, N_Z - dz) + min(dy, N_Y - dy)


FAR_FIRST = sorted(
    [(dz, dy) for dz in range(N_Z) for dy in range(N_Y) if dz or dy], key=lambda o: -hops(*o)
)
DP_FAR_FIRST = (4, 5, 3, 2, 6, 1, 7)


def wait_bytes(ref, sem):
    pltpu.make_async_copy(ref, ref, sem).wait()


def solve(m0, b1, b2, r1r1, r1w, ww, waw):
    g00, g01, g02 = m0, b1 - r1r1, b2 - r1w
    g11, g12, g22 = r1w + r1r1, ww + r1w, waw
    l10, l20 = g01 / g00, g02 / g00
    d1 = g11 - g01 * l10
    i1 = jnp.where(d1 > 1e-6 * g11, 1.0 / d1, 0.0)
    t = g12 - l20 * g01
    l21 = t * i1
    d2 = g22 - l20 * g02 - l21 * t
    i2 = jnp.where(d2 > 1e-6 * g22, 1.0 / d2, 0.0)
    z1 = b1 - l10 * m0
    z2 = b2 - l20 * m0 - l21 * z1
    y2 = z2 * i2
    y1 = z1 * i1 - l21 * y2
    y0 = 1.0 - l10 * y1 - l20 * y2
    return y0, y1, y2


def body(
    rows_all, cols_all,
    e_hbm, p_hbm, er_hbm, pc_hbm, g_hbm, o_emb, o_proto,
    ev, et, pv, er, pc, gv, kv, wv, td1, td2, td3, tp1, tp2, rs_out, rs_in,
    ef, eg, erc, kf, uf, sf, sp_out, sp_own, sp_in, sx,
    in_sem, ready, send, recv,
):
    dp, pr = lax.axis_index("dp"), lax.axis_index("proto")
    z, y = lax.div(pr, N_Y), lax.rem(pr, N_Y)
    cols = pv.shape[0]
    tiles = cols // LANES
    root_cols = math.sqrt(cols_all)
    root_rows = math.sqrt(rows_all)
    coupling = 1.0 / (root_rows * root_cols)

    loads = [
        pltpu.make_async_copy(src, dst, in_sem.at[i])
        for i, (src, dst) in enumerate(
            [(e_hbm, ev), (p_hbm, pv), (er_hbm, er), (pc_hbm, pc), (g_hbm, gv)]
        )
    ]
    for load in loads:
        load.start()

    barrier = pltpu.get_barrier_semaphore()
    for k in range(1, 8):
        pl.semaphore_signal(
            barrier, inc=1, device_id=(lax.rem(dp + k, N_DP), pr), device_id_type=MESH
        )
        pl.semaphore_signal(
            barrier, inc=1, device_id=(dp, z * N_Y + lax.rem(y + k, N_Y)), device_id_type=MESH
        )
        pl.semaphore_signal(
            barrier, inc=1, device_id=(dp, lax.rem(z + k, N_Z) * N_Y + y), device_id_type=MESH
        )
    for load in loads:
        load.wait()

    def to_dp(buf, i):
        for k in DP_FAR_FIRST:
            pltpu.make_async_remote_copy(
                src_ref=buf.at[dp], dst_ref=buf.at[dp], send_sem=send.at[i], recv_sem=recv.at[i],
                device_id=(lax.rem(dp + k, N_DP), pr), device_id_type=MESH,
            ).start()

    def to_proto(make, i):
        for dz, dy in FAR_FIRST:
            other = lax.rem(z + dz, N_Z) * N_Y + lax.rem(y + dy, N_Y)
            src, dst = make(other)
            pltpu.make_async_remote_copy(
                src_ref=src, dst_ref=dst, send_sem=send.at[i], recv_sem=recv.at[i],
                device_id=(dp, other), device_id_type=MESH,
            ).start()

    er_col = as_column(er[...])
    row_acc = jnp.zeros((LANES, LANES), F32)
    rhs_acc = jnp.zeros((LANES, LANES), F32)
    wide = 256
    er_wide = jnp.concatenate([er_col, er_col], axis=1)
    for c in range(cols // wide):
        at = pl.ds(c * wide, wide)
        scores = lax.dot_general(
            ev[...], pv[at, :], (((1,), (1,)), ((), ())), preferred_element_type=F32
        )
        k = jnp.exp(scores * (1.0 / TEMP) + er_wide + pc[:, at])
        kv[:, at] = k
        w = gv[:, at].astype(F32) * k
        td1[dp, 0:1, at] = jnp.sum(k, axis=0, keepdims=True)
        td1[dp, 1:2, at] = jnp.sum(w, axis=0, keepdims=True)
        row_acc += k[:, :LANES] + k[:, LANES:]
        rhs_acc += w[:, :LANES] + w[:, LANES:]
    td1[dp, 0:1, pl.ds(cols, LANES)] = er[...]
    td1[dp, 1:2, pl.ds(cols, LANES)] = er[...]
    mine = pl.ds(pl.multiple_of(dp * LANES, LANES), LANES)

    pl.semaphore_wait(barrier, 21)
    to_dp(td1, 0)
    for k in range(1, 8):
        pl.semaphore_signal(
            ready, inc=1, device_id=(dp, lax.rem(z + k, N_Z) * N_Y + y), device_id_type=MESH
        )
    row_part = as_row(row_acc)
    rhs_part = as_row(rhs_acc)

    for j in range(N_DP // 2):
        pair = ev[:, j * LANES : (j + 1) * LANES].astype(F32).T.astype(BF16)
        et[2 * j] = pair[:64]
        et[2 * j + 1] = pair[64:]
    wait_bytes(td1.at[pl.ds(0, N_DP - 1)], recv.at[0])
    col_pair = jnp.sum(td1[:, :, pl.ds(0, cols)], axis=0)
    dc = col_pair[0:1] * (1.0 / rows_all) + RIDGE
    v0c = col_pair[1:2] * (1.0 / root_rows)

    def lanes(row, t):
        return row[:, t * LANES : (t + 1) * LANES]

    def fold(row):
        return functools.reduce(lambda a, b: a + b, [lanes(row, t) for t in range(tiles)])

    def k_times(*vectors):
        accs = [jnp.zeros((LANES, LANES), F32) for _ in vectors]
        for t in range(tiles):
            k = kv[:, t * LANES : (t + 1) * LANES]
            accs = [a + k * lanes(v, t) for a, v in zip(accs, vectors)]
        return [as_row(a) for a in accs]

    (kv0,) = k_times(v0c)
    lane = lax.broadcasted_iota(jnp.int32, (1, LANES), 1)

    def by_two(row):
        return row + pltpu.roll(row, 64, 1)

    def by_four(row):
        row = by_two(row)
        return row + pltpu.roll(row, 32, 1)

    tp1[pr] = jnp.concatenate(
        [row_part, rhs_part, kv0,
         jnp.where(lane < 64, by_two(fold(v0c * v0c)), by_two(fold(v0c * dc * v0c)))],
        axis=0,
    )
    pl.semaphore_wait(ready, 7)
    to_proto(lambda other: (tp1.at[pr], tp1.at[pr]), 1)

    x, core = lax.div(dp, 2), lax.rem(dp, 2)
    sibling = 2 * x + 1 - core

    def block(d):
        return ef.at[pl.ds(pl.multiple_of(d * LANES, LANES), LANES)]

    for k in (2, 1, 3):
        pltpu.make_async_remote_copy(
            src_ref=ev, dst_ref=block(dp), send_sem=send.at[6], recv_sem=recv.at[6],
            device_id=(2 * lax.rem(x + k, 4) + core, pr), device_id_type=MESH,
        ).start()
    ef[mine, :] = ev[...]

    guess = col_pair[1:2] * (1.0 / rows_all) / dc
    for t in range(tiles):
        at = pl.ds(t * LANES, LANES)
        wv[:, at] = (kv[:, at] * (gv[:, at].astype(F32) - lanes(guess, t))).astype(BF16)

    def weighted_terms(to, first):
        lhs = jnp.concatenate([et[2 * j + first] for j in range(4)], axis=0)
        for c in range(cols // 512):
            at = pl.ds(c * 512, 512)
            part = jnp.dot(lhs, wv[:, at], preferred_element_type=F32).astype(BF16)
            for j in range(4):
                to[j, :, at] = part[64 * j : 64 * j + 64]

    weighted_terms(sp_out, 1 - core)
    pltpu.make_async_remote_copy(
        src_ref=sp_out, dst_ref=sp_in, send_sem=send.at[8], recv_sem=recv.at[8],
        device_id=(sibling, pr), device_id_type=MESH,
    ).start()
    weighted_terms(sp_own, core)
    for d in range(N_DP):
        erc[d * LANES : (d + 1) * LANES, :] = as_column(td1[d, 0:1, cols:])
    wait_bytes(tp1.at[pl.ds(0, N_PROTO - 1)], recv.at[1])
    one = jnp.sum(tp1[...], axis=0)
    dr = one[0:1] * (1.0 / cols_all) + RIDGE
    v0r = one[1:2] * (1.0 / root_cols)
    kv0 = one[2:3]
    s0 = total(jnp.where(lane < 64, one[3:4], 0.0))
    s1 = total(jnp.where(lane < 64, 0.0, one[3:4]))
    p_r = dr * v0r + coupling * kv0

    v0_col, p_col = as_column(v0r), as_column(p_r)
    for t in range(tiles):
        at = pl.ds(t * LANES, LANES)
        k = kv[:, at]
        td2[dp, 0:1, at] = jnp.sum(k * v0_col, axis=0, keepdims=True)
        td2[dp, 1:2, at] = jnp.sum(k * p_col, axis=0, keepdims=True)
    td2[dp, 0:1, pl.ds(cols, LANES)] = v0r * v0r
    td2[dp, 1:2, pl.ds(cols, LANES)] = v0r * (dr * v0r + (2.0 * coupling) * kv0)
    td2[dp, 0:1, pl.ds(cols + LANES, LANES)] = v0r
    td2[dp, 1:2, pl.ds(cols + LANES, LANES)] = p_r
    to_dp(td2, 2)

    def whole_kernel(c):
        at = pl.ds(c * wide, wide)
        scores = lax.dot_general(
            ef[...], pv[at, :], (((1,), (1,)), ((), ())), preferred_element_type=F32
        )
        shift = jnp.concatenate([erc[...], erc[...]], axis=1)
        kf[:, at] = jnp.exp(scores * (1.0 / TEMP) + shift + pc[:, at]).astype(BF16)

    wait_bytes(ef.at[pl.ds(0, 3 * LANES)], recv.at[6])
    for j in range(4):
        pltpu.make_async_remote_copy(
            src_ref=block(2 * j + core), dst_ref=block(2 * j + core),
            send_sem=send.at[7], recv_sem=recv.at[7],
            device_id=(sibling, pr), device_id_type=MESH,
        ).start()
    wait_bytes(sp_in, recv.at[8])
    for j in range(4):
        sp_own[j] = (sp_own[j].astype(F32) + sp_in[j].astype(F32)).astype(BF16)
    wait_bytes(td2.at[pl.ds(0, N_DP - 1)], recv.at[2])
    two = jnp.sum(td2[...], axis=0)
    m0 = s0 + total(two[0:1, cols : cols + LANES])
    m1 = s1 + total(two[1:2, cols : cols + LANES])
    theta = m1 / m0
    step = m0 / m1
    ktv0, ktp = two[0:1, :cols], two[1:2, :cols]
    r1r = v0r - step * p_r
    r1c = v0c - step * (dc * v0c + coupling * ktv0)
    ktr1 = ktv0 - step * ktp
    wc = step * (dc * r1c + coupling * ktr1) - r1c

    kr1, kw = k_times(r1c, wc)
    q = [by_four(fold(v)) for v in
         (r1c * r1c, r1c * wc, v0c * wc, wc * wc, wc * dc * wc, v0c * r1c)]
    tp2[pr] = jnp.concatenate(
        [kr1, kw,
         jnp.where(lane < 64, jnp.where(lane < 32, q[0], q[1]), jnp.where(lane < 96, q[2], q[3])),
         jnp.where(lane < 64, jnp.where(lane < 32, q[4], q[5]), 0.0)],
        axis=0,
    )
    to_proto(lambda other: (tp2.at[pr], tp2.at[pr]), 3)
    for k in (2, 1, 3):
        other = lax.rem(x + k, 4)
        pltpu.make_async_remote_copy(
            src_ref=sp_own.at[other], dst_ref=sx.at[x], send_sem=send.at[9], recv_sem=recv.at[9],
            device_id=(2 * other + core, pr), device_id_type=MESH,
        ).start()
    sx[x] = sp_own[x]
    wait_bytes(ef.at[pl.ds(0, 4 * LANES)], recv.at[7])
    for d in range(N_DP):
        eg[d] = ef[d * LANES : (d + 1) * LANES, pl.ds(pl.multiple_of(x * LANES, LANES), LANES)].astype(F32).T
    for c in range(cols // wide):
        whole_kernel(c)
    share = pl.ds(pl.multiple_of(64 * core, 64), 64)
    lhs = jnp.concatenate([eg[d, share, :] for d in range(N_DP)], axis=1).astype(BF16)
    for c in range(cols // 512):
        at = pl.ds(c * 512, 512)
        uf[:, at] = jnp.dot(lhs, kf[:, at], preferred_element_type=F32)
    wait_bytes(tp2.at[pl.ds(0, N_PROTO - 1)], recv.at[3])
    three = jnp.sum(tp2[...], axis=0)
    kr1, kw = three[0:1], three[1:2]
    wr = step * (dr * r1r + coupling * kr1) - r1r
    td3[dp] = jnp.concatenate(
        [r1r * r1r, r1r * wr, v0r * wr, wr * wr, wr * (dr * wr + (2.0 * coupling) * kw), v0r * r1r,
         wr, jnp.zeros((1, LANES), F32)],
        axis=0,
    )
    to_dp(td3, 4)
    wait_bytes(sx.at[pl.ds(0, 3)], recv.at[9])
    for c in range(cols // 512):
        at = pl.ds(c * 512, 512)
        acc = sx[0, :, at].astype(F32)
        for j in range(1, 4):
            acc += sx[j, :, at].astype(F32)
        sf[:, at] = acc
    wait_bytes(td3.at[pl.ds(0, N_DP - 1)], recv.at[4])
    four = total(jnp.sum(td3[...], axis=0))
    five = [
        total(jnp.where((lane >= 32 * g) & (lane < 32 * g + 32), three[r : r + 1], 0.0))
        for r, g in ((2, 0), (2, 1), (2, 2), (2, 3), (3, 0), (3, 1))
    ]
    r1r1, r1w, v0w = four[0:1] + five[0], four[1:2] + five[1], four[2:3] + five[2]
    ww, waw, v0r1 = four[3:4] + five[3], (four[4:5] + five[4]) * step, four[5:6] + five[5]
    y0, y1, y2 = solve(m0, v0r1, v0w, r1r1, r1w, ww, waw)
    y0, y1, y2 = y0 * step, y1 * step, y2 * step
    sol_r = (y0 * v0r + y1 * r1r + y2 * wr) * (1.0 / root_cols)
    sol_c = (y0 * v0c + y1 * r1c + y2 * wc) * (1.0 / root_rows)

    sol_col = as_column(sol_r)
    for t in range(tiles):
        at = pl.ds(t * LANES, LANES)
        g = gv[:, at].astype(F32)
        wv[:, at] = (kv[:, at] * (g - sol_col - lanes(sol_c, t)) * (1.0 / TEMP)).astype(BF16)
    ge = jnp.dot(wv[...], pv[...], preferred_element_type=F32)
    for j in range(4):
        rs_out[pl.ds(16 * j, 16)] = ge[:, j * LANES : (j + 1) * LANES].T.reshape(16, 8, LANES).astype(BF16)
    to_proto(lambda other: (rs_out.at[other], rs_in.at[pr]), 5)
    rs_in[pr] = rs_out[pr]

    scaled = []
    for d in range(N_DP):
        v0d = td2[d, 0:1, pl.ds(cols + LANES, LANES)]
        r1d = v0d - step * td2[d, 1:2, pl.ds(cols + LANES, LANES)]
        sol_d = (y0 * v0d + y1 * r1d + y2 * td3[d, 6:7, :]) * (1.0 / root_cols)
        scaled.append((eg[d, share, :] * sol_d).astype(BF16))
    lhs = jnp.concatenate(scaled, axis=1)
    for c in range(cols // 512):
        at = pl.ds(c * 512, 512)
        terms = jnp.dot(lhs, kf[:, at], preferred_element_type=F32)
        part = sf[:, at] - terms - uf[:, at] * (sol_c - guess)[:, c * 512 : (c + 1) * 512]
        o_proto[:, at] = (part * (1.0 / TEMP)).astype(BF16)
    wait_bytes(rs_in.at[pl.ds(0, N_PROTO - 1)], recv.at[5])
    o_emb[...] = jnp.sum(rs_in[...].astype(F32), axis=0)

    wait_bytes(td1.at[pl.ds(0, N_DP - 1)], send.at[0])
    wait_bytes(tp1.at[pl.ds(0, N_PROTO - 1)], send.at[1])
    wait_bytes(td2.at[pl.ds(0, N_DP - 1)], send.at[2])
    wait_bytes(tp2.at[pl.ds(0, N_PROTO - 1)], send.at[3])
    wait_bytes(td3.at[pl.ds(0, N_DP - 1)], send.at[4])
    wait_bytes(rs_out.at[pl.ds(0, N_PROTO - 1)], send.at[5])
    wait_bytes(ef.at[pl.ds(0, 3 * LANES)], send.at[6])
    wait_bytes(ef.at[pl.ds(0, 4 * LANES)], send.at[7])
    wait_bytes(sp_out, send.at[8])
    wait_bytes(sp_own.at[pl.ds(0, 3)], send.at[9])


def shards(
    embeddings, prototypes, embedding_log_potential, prototype_log_potential, scaled_plan_gradient
):
    rows, width = embeddings.shape
    cols = prototypes.shape[0]
    share = width // N_DP
    any_space = pl.BlockSpec(memory_space=pl.ANY)
    vmem = pl.BlockSpec(memory_space=pltpu.VMEM)
    ge, gp = pl.pallas_call(
        functools.partial(body, rows * N_DP, cols * N_PROTO),
        out_shape=(
            jax.ShapeDtypeStruct((width // N_PROTO, rows), F32),
            jax.ShapeDtypeStruct((share, cols), BF16),
        ),
        in_specs=[any_space] * 5,
        out_specs=(vmem, vmem),
        scratch_shapes=[
            pltpu.VMEM((rows, width), BF16),
            pltpu.VMEM((N_DP, share, rows), BF16),
            pltpu.VMEM((cols, width), BF16),
            pltpu.VMEM((1, rows), F32),
            pltpu.VMEM((1, cols), F32),
            pltpu.VMEM((rows, cols), BF16),
            pltpu.VMEM((rows, cols), F32),
            pltpu.VMEM((rows, cols), BF16),
            pltpu.VMEM((N_DP, 2, cols + LANES), F32),
            pltpu.VMEM((N_DP, 2, cols + 2 * LANES), F32),
            pltpu.VMEM((N_DP, 8, LANES), F32),
            pltpu.VMEM((N_PROTO, 4, LANES), F32),
            pltpu.VMEM((N_PROTO, 4, LANES), F32),
            pltpu.VMEM((N_PROTO, 8, LANES), BF16),
            pltpu.VMEM((N_PROTO, 8, LANES), BF16),
            pltpu.VMEM((rows * N_DP, width), BF16),
            pltpu.VMEM((N_DP, LANES, rows), F32),
            pltpu.VMEM((rows * N_DP, LANES), F32),
            pltpu.VMEM((rows * N_DP, cols), BF16),
            pltpu.VMEM((share, cols), F32),
            pltpu.VMEM((share, cols), F32),
            pltpu.VMEM((4, share, cols), BF16),
            pltpu.VMEM((4, share, cols), BF16),
            pltpu.VMEM((4, share, cols), BF16),
            pltpu.VMEM((4, share, cols), BF16),
            pltpu.SemaphoreType.DMA((5,)),
            pltpu.SemaphoreType.REGULAR,
            pltpu.SemaphoreType.DMA((10,)),
            pltpu.SemaphoreType.DMA((10,)),
        ],
        compiler_params=pltpu.CompilerParams(
            collective_id=0, has_side_effects=True, vmem_limit_bytes=56 * 1024 * 1024
        ),
    )(
        embeddings,
        prototypes,
        embedding_log_potential.reshape(1, rows),
        prototype_log_potential.reshape(1, cols),
        scaled_plan_gradient,
    )
    return ge.T, gp.T


def solution(mesh):
    return jax.shard_map(
        shards,
        mesh=mesh,
        in_specs=(P("dp", None), P("proto", None), P("dp"), P("proto"), P("dp", "proto")),
        out_specs=(P("dp", "proto"), P("proto", "dp")),
        check_vma=False,
    )
```

```python
import functools
import math

import jax
import jax.numpy as jnp
from jax import lax
from jax.experimental import pallas as pl
from jax.experimental.pallas import tpu as pltpu
from jax.sharding import PartitionSpec as P

MESH = pl.DeviceIdType.MESH
TEMP = 0.05
RIDGE = 0.05
N_DP = 8
N_Z = 8
N_Y = 8
N_PROTO = N_Z * N_Y
LANES = 128
F32 = jnp.float32
BF16 = jnp.bfloat16


def total(values):
    return jnp.sum(values, axis=1, keepdims=True)


def as_column(row):
    return jnp.broadcast_to(row, (LANES, LANES)).T


def as_row(acc):
    return jnp.sum(acc.T, axis=0, keepdims=True)


def hops(dz, dy):
    return min(dz, N_Z - dz) + min(dy, N_Y - dy)


FAR_FIRST = sorted(
    [(dz, dy) for dz in range(N_Z) for dy in range(N_Y) if dz or dy], key=lambda o: -hops(*o)
)
DP_FAR_FIRST = (4, 5, 3, 2, 6, 1, 7)


def wait_bytes(ref, sem):
    pltpu.make_async_copy(ref, ref, sem).wait()


def solve(m0, b1, b2, r1r1, r1w, ww, waw):
    g00, g01, g02 = m0, b1 - r1r1, b2 - r1w
    g11, g12, g22 = r1w + r1r1, ww + r1w, waw
    l10, l20 = g01 / g00, g02 / g00
    d1 = g11 - g01 * l10
    i1 = jnp.where(d1 > 1e-6 * g11, 1.0 / d1, 0.0)
    t = g12 - l20 * g01
    l21 = t * i1
    d2 = g22 - l20 * g02 - l21 * t
    i2 = jnp.where(d2 > 1e-6 * g22, 1.0 / d2, 0.0)
    z1 = b1 - l10 * m0
    z2 = b2 - l20 * m0 - l21 * z1
    y2 = z2 * i2
    y1 = z1 * i1 - l21 * y2
    y0 = 1.0 - l10 * y1 - l20 * y2
    return y0, y1, y2


def body(
    rows_all, cols_all,
    e_hbm, p_hbm, er_hbm, pc_hbm, g_hbm, o_emb, o_proto,
    ev, et, pv, er, pc, gv, kv, wv, td1, td2, td3, tp1, tp2, rs_out, rs_in,
    ef, eg, erc, kf, uf, sf, sp_out, sp_own, sp_in, s2, sx,
    in_sem, ready, send, recv,
):
    dp, pr = lax.axis_index("dp"), lax.axis_index("proto")
    z, y = lax.div(pr, N_Y), lax.rem(pr, N_Y)
    cols = pv.shape[0]
    tiles = cols // LANES
    root_cols = math.sqrt(cols_all)
    root_rows = math.sqrt(rows_all)
    coupling = 1.0 / (root_rows * root_cols)

    loads = [
        pltpu.make_async_copy(src, dst, in_sem.at[i])
        for i, (src, dst) in enumerate(
            [(e_hbm, ev), (p_hbm, pv), (er_hbm, er), (pc_hbm, pc), (g_hbm, gv)]
        )
    ]
    for load in loads:
        load.start()

    barrier = pltpu.get_barrier_semaphore()
    for k in range(1, 8):
        pl.semaphore_signal(
            barrier, inc=1, device_id=(lax.rem(dp + k, N_DP), pr), device_id_type=MESH
        )
        pl.semaphore_signal(
            barrier, inc=1, device_id=(dp, z * N_Y + lax.rem(y + k, N_Y)), device_id_type=MESH
        )
        pl.semaphore_signal(
            barrier, inc=1, device_id=(dp, lax.rem(z + k, N_Z) * N_Y + y), device_id_type=MESH
        )
    for load in loads:
        load.wait()

    def to_dp(buf, i):
        for k in DP_FAR_FIRST:
            pltpu.make_async_remote_copy(
                src_ref=buf.at[dp], dst_ref=buf.at[dp], send_sem=send.at[i], recv_sem=recv.at[i],
                device_id=(lax.rem(dp + k, N_DP), pr), device_id_type=MESH,
            ).start()

    def to_proto(make, i):
        for dz, dy in FAR_FIRST:
            other = lax.rem(z + dz, N_Z) * N_Y + lax.rem(y + dy, N_Y)
            src, dst = make(other)
            pltpu.make_async_remote_copy(
                src_ref=src, dst_ref=dst, send_sem=send.at[i], recv_sem=recv.at[i],
                device_id=(dp, other), device_id_type=MESH,
            ).start()

    er_col = as_column(er[...])
    row_acc = jnp.zeros((LANES, LANES), F32)
    rhs_acc = jnp.zeros((LANES, LANES), F32)
    wide = 256
    er_wide = jnp.concatenate([er_col, er_col], axis=1)
    for c in range(cols // wide):
        at = pl.ds(c * wide, wide)
        scores = lax.dot_general(
            ev[...], pv[at, :], (((1,), (1,)), ((), ())), preferred_element_type=F32
        )
        k = jnp.exp(scores * (1.0 / TEMP) + er_wide + pc[:, at])
        kv[:, at] = k
        w = gv[:, at].astype(F32) * k
        td1[dp, 0:1, at] = jnp.sum(k, axis=0, keepdims=True)
        td1[dp, 1:2, at] = jnp.sum(w, axis=0, keepdims=True)
        row_acc += k[:, :LANES] + k[:, LANES:]
        rhs_acc += w[:, :LANES] + w[:, LANES:]
    td1[dp, 0:1, pl.ds(cols, LANES)] = er[...]
    td1[dp, 1:2, pl.ds(cols, LANES)] = er[...]
    mine = pl.ds(pl.multiple_of(dp * LANES, LANES), LANES)

    pl.semaphore_wait(barrier, 21)
    to_dp(td1, 0)
    for k in range(1, 8):
        pl.semaphore_signal(
            ready, inc=1, device_id=(dp, lax.rem(z + k, N_Z) * N_Y + y), device_id_type=MESH
        )
    row_part = as_row(row_acc)
    rhs_part = as_row(rhs_acc)

    for j in range(N_DP // 2):
        pair = ev[:, j * LANES : (j + 1) * LANES].astype(F32).T.astype(BF16)
        et[2 * j] = pair[:64]
        et[2 * j + 1] = pair[64:]
    wait_bytes(td1.at[pl.ds(0, N_DP - 1)], recv.at[0])
    col_pair = jnp.sum(td1[:, :, pl.ds(0, cols)], axis=0)
    dc = col_pair[0:1] * (1.0 / rows_all) + RIDGE
    v0c = col_pair[1:2] * (1.0 / root_rows)

    def lanes(row, t):
        return row[:, t * LANES : (t + 1) * LANES]

    def fold(row):
        return functools.reduce(lambda a, b: a + b, [lanes(row, t) for t in range(tiles)])

    def k_times(*vectors):
        accs = [jnp.zeros((LANES, LANES), F32) for _ in vectors]
        for t in range(tiles):
            k = kv[:, t * LANES : (t + 1) * LANES]
            accs = [a + k * lanes(v, t) for a, v in zip(accs, vectors)]
        return [as_row(a) for a in accs]

    (kv0,) = k_times(v0c)
    lane = lax.broadcasted_iota(jnp.int32, (1, LANES), 1)

    def by_two(row):
        return row + pltpu.roll(row, 64, 1)

    def by_four(row):
        row = by_two(row)
        return row + pltpu.roll(row, 32, 1)

    tp1[pr] = jnp.concatenate(
        [row_part, rhs_part, kv0,
         jnp.where(lane < 64, by_two(fold(v0c * v0c)), by_two(fold(v0c * dc * v0c)))],
        axis=0,
    )
    pl.semaphore_wait(ready, 7)
    to_proto(lambda other: (tp1.at[pr], tp1.at[pr]), 1)

    x, core = lax.div(dp, 2), lax.rem(dp, 2)
    sibling = 2 * x + 1 - core

    def block(d):
        return ef.at[pl.ds(pl.multiple_of(d * LANES, LANES), LANES)]

    for k in (2, 1, 3):
        pltpu.make_async_remote_copy(
            src_ref=ev, dst_ref=block(dp), send_sem=send.at[6], recv_sem=recv.at[6],
            device_id=(2 * lax.rem(x + k, 4) + core, pr), device_id_type=MESH,
        ).start()
    ef[mine, :] = ev[...]

    guess = col_pair[1:2] * (1.0 / rows_all) / dc
    for t in range(tiles):
        at = pl.ds(t * LANES, LANES)
        wv[:, at] = (kv[:, at] * (gv[:, at].astype(F32) - lanes(guess, t))).astype(BF16)

    def weighted_terms(to, first):
        lhs = jnp.concatenate([et[2 * j + first] for j in range(4)], axis=0)
        for c in range(cols // 512):
            at = pl.ds(c * 512, 512)
            part = jnp.dot(lhs, wv[:, at], preferred_element_type=F32).astype(BF16)
            for j in range(4):
                to[j, :, at] = part[64 * j : 64 * j + 64]

    weighted_terms(sp_out, 1 - core)
    pltpu.make_async_remote_copy(
        src_ref=sp_out, dst_ref=sp_in, send_sem=send.at[8], recv_sem=recv.at[8],
        device_id=(sibling, pr), device_id_type=MESH,
    ).start()
    weighted_terms(sp_own, core)
    for d in range(N_DP):
        erc[d * LANES : (d + 1) * LANES, :] = as_column(td1[d, 0:1, cols:])
    wait_bytes(tp1.at[pl.ds(0, N_PROTO - 1)], recv.at[1])
    one = jnp.sum(tp1[...], axis=0)
    dr = one[0:1] * (1.0 / cols_all) + RIDGE
    v0r = one[1:2] * (1.0 / root_cols)
    kv0 = one[2:3]
    s0 = total(jnp.where(lane < 64, one[3:4], 0.0))
    s1 = total(jnp.where(lane < 64, 0.0, one[3:4]))
    p_r = dr * v0r + coupling * kv0

    v0_col, p_col = as_column(v0r), as_column(p_r)
    for t in range(tiles):
        at = pl.ds(t * LANES, LANES)
        k = kv[:, at]
        td2[dp, 0:1, at] = jnp.sum(k * v0_col, axis=0, keepdims=True)
        td2[dp, 1:2, at] = jnp.sum(k * p_col, axis=0, keepdims=True)
    td2[dp, 0:1, pl.ds(cols, LANES)] = v0r * v0r
    td2[dp, 1:2, pl.ds(cols, LANES)] = v0r * (dr * v0r + (2.0 * coupling) * kv0)
    td2[dp, 0:1, pl.ds(cols + LANES, LANES)] = v0r
    td2[dp, 1:2, pl.ds(cols + LANES, LANES)] = p_r
    to_dp(td2, 2)

    def whole_kernel(c):
        at = pl.ds(c * wide, wide)
        scores = lax.dot_general(
            ef[...], pv[at, :], (((1,), (1,)), ((), ())), preferred_element_type=F32
        )
        shift = jnp.concatenate([erc[...], erc[...]], axis=1)
        kf[:, at] = jnp.exp(scores * (1.0 / TEMP) + shift + pc[:, at]).astype(BF16)

    wait_bytes(ef.at[pl.ds(0, 3 * LANES)], recv.at[6])
    for j in range(4):
        pltpu.make_async_remote_copy(
            src_ref=block(2 * j + core), dst_ref=block(2 * j + core),
            send_sem=send.at[7], recv_sem=recv.at[7],
            device_id=(sibling, pr), device_id_type=MESH,
        ).start()
    wait_bytes(sp_in, recv.at[8])
    for j in range(4):
        sp_own[j] = (sp_own[j].astype(F32) + sp_in[j].astype(F32)).astype(BF16)
    right, left, across = (lax.rem(x + k, 4) for k in (1, 3, 2))
    for i, to in enumerate((right, left)):
        pltpu.make_async_remote_copy(
            src_ref=sp_own.at[across, pl.ds(32 * i, 32)], dst_ref=s2.at[i],
            send_sem=send.at[9], recv_sem=recv.at[9],
            device_id=(2 * to + core, pr), device_id_type=MESH,
        ).start()
    wait_bytes(td2.at[pl.ds(0, N_DP - 1)], recv.at[2])
    two = jnp.sum(td2[...], axis=0)
    m0 = s0 + total(two[0:1, cols : cols + LANES])
    m1 = s1 + total(two[1:2, cols : cols + LANES])
    theta = m1 / m0
    step = m0 / m1
    ktv0, ktp = two[0:1, :cols], two[1:2, :cols]
    r1r = v0r - step * p_r
    r1c = v0c - step * (dc * v0c + coupling * ktv0)
    ktr1 = ktv0 - step * ktp
    wc = step * (dc * r1c + coupling * ktr1) - r1c

    kr1, kw = k_times(r1c, wc)
    q = [by_four(fold(v)) for v in
         (r1c * r1c, r1c * wc, v0c * wc, wc * wc, wc * dc * wc, v0c * r1c)]
    tp2[pr] = jnp.concatenate(
        [kr1, kw,
         jnp.where(lane < 64, jnp.where(lane < 32, q[0], q[1]), jnp.where(lane < 96, q[2], q[3])),
         jnp.where(lane < 64, jnp.where(lane < 32, q[4], q[5]), 0.0)],
        axis=0,
    )
    to_proto(lambda other: (tp2.at[pr], tp2.at[pr]), 3)
    wait_bytes(s2, recv.at[9])
    for i, to in enumerate((right, left)):
        half = pl.ds(32 * i, 32)
        sp_own[to, half] = (sp_own[to, half].astype(F32) + s2[i].astype(F32)).astype(BF16)
        pltpu.make_async_remote_copy(
            src_ref=sp_own.at[to], dst_ref=sx.at[i], send_sem=send.at[10], recv_sem=recv.at[10],
            device_id=(2 * to + core, pr), device_id_type=MESH,
        ).start()
    wait_bytes(ef.at[pl.ds(0, 4 * LANES)], recv.at[7])
    for d in range(N_DP):
        eg[d] = ef[d * LANES : (d + 1) * LANES, pl.ds(pl.multiple_of(x * LANES, LANES), LANES)].astype(F32).T
    for c in range(cols // wide):
        whole_kernel(c)
    share = pl.ds(pl.multiple_of(64 * core, 64), 64)
    lhs = jnp.concatenate([eg[d, share, :] for d in range(N_DP)], axis=1).astype(BF16)
    for c in range(cols // 512):
        at = pl.ds(c * 512, 512)
        uf[:, at] = jnp.dot(lhs, kf[:, at], preferred_element_type=F32)
    wait_bytes(tp2.at[pl.ds(0, N_PROTO - 1)], recv.at[3])
    three = jnp.sum(tp2[...], axis=0)
    kr1, kw = three[0:1], three[1:2]
    wr = step * (dr * r1r + coupling * kr1) - r1r
    td3[dp] = jnp.concatenate(
        [r1r * r1r, r1r * wr, v0r * wr, wr * wr, wr * (dr * wr + (2.0 * coupling) * kw), v0r * r1r,
         wr, jnp.zeros((1, LANES), F32)],
        axis=0,
    )
    to_dp(td3, 4)
    five = [
        total(jnp.where((lane >= 32 * g) & (lane < 32 * g + 32), three[r : r + 1], 0.0))
        for r, g in ((2, 0), (2, 1), (2, 2), (2, 3), (3, 0), (3, 1))
    ]
    sol_cols = [as_column(v) for v in (v0r, r1r, wr)]
    wait_bytes(td3.at[pl.ds(0, N_DP - 1)], recv.at[4])
    four = total(jnp.sum(td3[...], axis=0))
    r1r1, r1w, v0w = four[0:1] + five[0], four[1:2] + five[1], four[2:3] + five[2]
    ww, waw, v0r1 = four[3:4] + five[3], (four[4:5] + five[4]) * step, four[5:6] + five[5]
    y0, y1, y2 = solve(m0, v0r1, v0w, r1r1, r1w, ww, waw)
    y0, y1, y2 = y0 * step, y1 * step, y2 * step
    sol_c = (y0 * v0c + y1 * r1c + y2 * wc) * (1.0 / root_rows)

    ys = [v * (1.0 / root_cols) for v in (y0, y1, y2)]
    sol_col = ys[0] * sol_cols[0] + ys[1] * sol_cols[1] + ys[2] * sol_cols[2]
    for t in range(tiles):
        at = pl.ds(t * LANES, LANES)
        g = gv[:, at].astype(F32)
        wv[:, at] = (kv[:, at] * (g - sol_col - lanes(sol_c, t)) * (1.0 / TEMP)).astype(BF16)
    ge = jnp.dot(wv[...], pv[...], preferred_element_type=F32)
    for j in range(4):
        rs_out[pl.ds(16 * j, 16)] = ge[:, j * LANES : (j + 1) * LANES].T.reshape(16, 8, LANES).astype(BF16)
    to_proto(lambda other: (rs_out.at[other], rs_in.at[pr]), 5)
    rs_in[pr] = rs_out[pr]
    wait_bytes(sx, recv.at[10])
    for c in range(cols // 512):
        at = pl.ds(c * 512, 512)
        both = sx[0, :, at].astype(F32) + sx[1, :, at].astype(F32)
        sf[:, at] = sp_own[x, :, at].astype(F32) + both

    scaled = []
    for d in range(N_DP):
        v0d = td2[d, 0:1, pl.ds(cols + LANES, LANES)]
        r1d = v0d - step * td2[d, 1:2, pl.ds(cols + LANES, LANES)]
        sol_d = (y0 * v0d + y1 * r1d + y2 * td3[d, 6:7, :]) * (1.0 / root_cols)
        scaled.append((eg[d, share, :] * sol_d).astype(BF16))
    lhs = jnp.concatenate(scaled, axis=1)
    for c in range(cols // 512):
        at = pl.ds(c * 512, 512)
        terms = jnp.dot(lhs, kf[:, at], preferred_element_type=F32)
        part = sf[:, at] - terms - uf[:, at] * (sol_c - guess)[:, c * 512 : (c + 1) * 512]
        o_proto[:, at] = (part * (1.0 / TEMP)).astype(BF16)
    wait_bytes(rs_in.at[pl.ds(0, N_PROTO - 1)], recv.at[5])
    o_emb[...] = jnp.sum(rs_in[...].astype(F32), axis=0)

    wait_bytes(td1.at[pl.ds(0, N_DP - 1)], send.at[0])
    wait_bytes(tp1.at[pl.ds(0, N_PROTO - 1)], send.at[1])
    wait_bytes(td2.at[pl.ds(0, N_DP - 1)], send.at[2])
    wait_bytes(tp2.at[pl.ds(0, N_PROTO - 1)], send.at[3])
    wait_bytes(td3.at[pl.ds(0, N_DP - 1)], send.at[4])
    wait_bytes(rs_out.at[pl.ds(0, N_PROTO - 1)], send.at[5])
    wait_bytes(ef.at[pl.ds(0, 3 * LANES)], send.at[6])
    wait_bytes(ef.at[pl.ds(0, 4 * LANES)], send.at[7])
    wait_bytes(sp_out, send.at[8])
    wait_bytes(s2, send.at[9])
    wait_bytes(sx, send.at[10])


def shards(
    embeddings, prototypes, embedding_log_potential, prototype_log_potential, scaled_plan_gradient
):
    rows, width = embeddings.shape
    cols = prototypes.shape[0]
    share = width // N_DP
    any_space = pl.BlockSpec(memory_space=pl.ANY)
    vmem = pl.BlockSpec(memory_space=pltpu.VMEM)
    ge, gp = pl.pallas_call(
        functools.partial(body, rows * N_DP, cols * N_PROTO),
        out_shape=(
            jax.ShapeDtypeStruct((width // N_PROTO, rows), F32),
            jax.ShapeDtypeStruct((share, cols), BF16),
        ),
        in_specs=[any_space] * 5,
        out_specs=(vmem, vmem),
        scratch_shapes=[
            pltpu.VMEM((rows, width), BF16),
            pltpu.VMEM((N_DP, share, rows), BF16),
            pltpu.VMEM((cols, width), BF16),
            pltpu.VMEM((1, rows), F32),
            pltpu.VMEM((1, cols), F32),
            pltpu.VMEM((rows, cols), BF16),
            pltpu.VMEM((rows, cols), F32),
            pltpu.VMEM((rows, cols), BF16),
            pltpu.VMEM((N_DP, 2, cols + LANES), F32),
            pltpu.VMEM((N_DP, 2, cols + 2 * LANES), F32),
            pltpu.VMEM((N_DP, 8, LANES), F32),
            pltpu.VMEM((N_PROTO, 4, LANES), F32),
            pltpu.VMEM((N_PROTO, 4, LANES), F32),
            pltpu.VMEM((N_PROTO, 8, LANES), BF16),
            pltpu.VMEM((N_PROTO, 8, LANES), BF16),
            pltpu.VMEM((rows * N_DP, width), BF16),
            pltpu.VMEM((N_DP, LANES, rows), F32),
            pltpu.VMEM((rows * N_DP, LANES), F32),
            pltpu.VMEM((rows * N_DP, cols), BF16),
            pltpu.VMEM((share, cols), F32),
            pltpu.VMEM((share, cols), F32),
            pltpu.VMEM((4, share, cols), BF16),
            pltpu.VMEM((4, share, cols), BF16),
            pltpu.VMEM((4, share, cols), BF16),
            pltpu.VMEM((2, share // 2, cols), BF16),
            pltpu.VMEM((2, share, cols), BF16),
            pltpu.SemaphoreType.DMA((5,)),
            pltpu.SemaphoreType.REGULAR,
            pltpu.SemaphoreType.DMA((11,)),
            pltpu.SemaphoreType.DMA((11,)),
        ],
        compiler_params=pltpu.CompilerParams(
            collective_id=0, has_side_effects=True, vmem_limit_bytes=56 * 1024 * 1024
        ),
    )(
        embeddings,
        prototypes,
        embedding_log_potential.reshape(1, rows),
        prototype_log_potential.reshape(1, cols),
        scaled_plan_gradient,
    )
    return ge.T, gp.T


def solution(mesh):
    return jax.shard_map(
        shards,
        mesh=mesh,
        in_specs=(P("dp", None), P("proto", None), P("dp"), P("proto"), P("dp", "proto")),
        out_specs=(P("dp", "proto"), P("proto", "dp")),
        check_vma=False,
    )
```

```python
import functools
import math

import jax
import jax.numpy as jnp
from jax import lax
from jax.experimental import pallas as pl
from jax.experimental.pallas import tpu as pltpu
from jax.sharding import PartitionSpec as P

MESH = pl.DeviceIdType.MESH
TEMP = 0.05
RIDGE = 0.05
N_DP = 8
N_Z = 8
N_Y = 8
N_PROTO = N_Z * N_Y
LANES = 128
F32 = jnp.float32
BF16 = jnp.bfloat16


def total(values):
    return jnp.sum(values, axis=1, keepdims=True)


def as_column(row):
    return jnp.broadcast_to(row, (LANES, LANES)).T


def as_row(acc):
    return jnp.sum(acc.T, axis=0, keepdims=True)


def hops(dz, dy):
    return min(dz, N_Z - dz) + min(dy, N_Y - dy)


FAR_FIRST = sorted(
    [(dz, dy) for dz in range(N_Z) for dy in range(N_Y) if dz or dy], key=lambda o: -hops(*o)
)
DP_FAR_FIRST = (4, 5, 3, 2, 6, 1, 7)
FAR = (4, 3, 5, 2, 6, 1, 7)


def wait_bytes(ref, sem):
    pltpu.make_async_copy(ref, ref, sem).wait()


def solve(m0, b1, b2, r1r1, r1w, ww, waw):
    g00, g01, g02 = m0, b1 - r1r1, b2 - r1w
    g11, g12, g22 = r1w + r1r1, ww + r1w, waw
    l10, l20 = g01 / g00, g02 / g00
    d1 = g11 - g01 * l10
    i1 = jnp.where(d1 > 1e-6 * g11, 1.0 / d1, 0.0)
    t = g12 - l20 * g01
    l21 = t * i1
    d2 = g22 - l20 * g02 - l21 * t
    i2 = jnp.where(d2 > 1e-6 * g22, 1.0 / d2, 0.0)
    z1 = b1 - l10 * m0
    z2 = b2 - l20 * m0 - l21 * z1
    y2 = z2 * i2
    y1 = z1 * i1 - l21 * y2
    y0 = 1.0 - l10 * y1 - l20 * y2
    return y0, y1, y2


def body(
    rows_all, cols_all,
    e_hbm, p_hbm, er_hbm, pc_hbm, g_hbm, o_emb, o_proto,
    ev, et, pv, er, pc, gv, kv, wv, td1, td2, td3, tp1, tp2, rs_out, rs_in,
    ef, eg, erc, kf, uf, sf, sp_out, sp_own, sp_in, s2, sx,
    in_sem, ready, send, recv,
):
    dp, pr = lax.axis_index("dp"), lax.axis_index("proto")
    z, y = lax.div(pr, N_Y), lax.rem(pr, N_Y)
    cols = pv.shape[0]
    tiles = cols // LANES
    root_cols = math.sqrt(cols_all)
    root_rows = math.sqrt(rows_all)
    coupling = 1.0 / (root_rows * root_cols)

    loads = [
        pltpu.make_async_copy(src, dst, in_sem.at[i])
        for i, (src, dst) in enumerate(
            [(e_hbm, ev), (p_hbm, pv), (er_hbm, er), (pc_hbm, pc), (g_hbm, gv)]
        )
    ]
    for load in loads:
        load.start()

    barrier = pltpu.get_barrier_semaphore()
    for k in FAR:
        pl.semaphore_signal(
            barrier, inc=1, device_id=(dp, z * N_Y + lax.rem(y + k, N_Y)), device_id_type=MESH
        )
        pl.semaphore_signal(
            barrier, inc=1, device_id=(dp, lax.rem(z + k, N_Z) * N_Y + y), device_id_type=MESH
        )
    for k in DP_FAR_FIRST:
        pl.semaphore_signal(
            barrier, inc=1, device_id=(lax.rem(dp + k, N_DP), pr), device_id_type=MESH
        )
    for load in loads:
        load.wait()

    def to_dp(buf, i):
        for k in DP_FAR_FIRST:
            pltpu.make_async_remote_copy(
                src_ref=buf.at[dp], dst_ref=buf.at[dp], send_sem=send.at[i], recv_sem=recv.at[i],
                device_id=(lax.rem(dp + k, N_DP), pr), device_id_type=MESH,
            ).start()

    def to_proto(make, i):
        for dz, dy in FAR_FIRST:
            other = lax.rem(z + dz, N_Z) * N_Y + lax.rem(y + dy, N_Y)
            src, dst = make(other)
            pltpu.make_async_remote_copy(
                src_ref=src, dst_ref=dst, send_sem=send.at[i], recv_sem=recv.at[i],
                device_id=(dp, other), device_id_type=MESH,
            ).start()

    er_col = as_column(er[...])
    row_acc = jnp.zeros((LANES, LANES), F32)
    rhs_acc = jnp.zeros((LANES, LANES), F32)
    wide = 256
    er_wide = jnp.concatenate([er_col, er_col], axis=1)
    for c in range(cols // wide):
        at = pl.ds(c * wide, wide)
        scores = lax.dot_general(
            ev[...], pv[at, :], (((1,), (1,)), ((), ())), preferred_element_type=F32
        )
        k = jnp.exp(scores * (1.0 / TEMP) + er_wide + pc[:, at])
        kv[:, at] = k
        w = gv[:, at].astype(F32) * k
        td1[dp, 0:1, at] = jnp.sum(k, axis=0, keepdims=True)
        td1[dp, 1:2, at] = jnp.sum(w, axis=0, keepdims=True)
        row_acc += k[:, :LANES] + k[:, LANES:]
        rhs_acc += w[:, :LANES] + w[:, LANES:]
    td1[dp, 0:1, pl.ds(cols, LANES)] = er[...]
    td1[dp, 1:2, pl.ds(cols, LANES)] = er[...]
    mine = pl.ds(pl.multiple_of(dp * LANES, LANES), LANES)

    pl.semaphore_wait(barrier, 21)
    to_dp(td1, 0)
    for k in FAR:
        pl.semaphore_signal(
            ready, inc=1, device_id=(dp, lax.rem(z + k, N_Z) * N_Y + y), device_id_type=MESH
        )
    row_part = as_row(row_acc)
    rhs_part = as_row(rhs_acc)

    for j in range(N_DP // 2):
        pair = ev[:, j * LANES : (j + 1) * LANES].astype(F32).T.astype(BF16)
        et[2 * j] = pair[:64]
        et[2 * j + 1] = pair[64:]
    wait_bytes(td1.at[pl.ds(0, N_DP - 1)], recv.at[0])
    col_pair = jnp.sum(td1[:, :, pl.ds(0, cols)], axis=0)
    dc = col_pair[0:1] * (1.0 / rows_all) + RIDGE
    v0c = col_pair[1:2] * (1.0 / root_rows)

    def lanes(row, t):
        return row[:, t * LANES : (t + 1) * LANES]

    def fold(row):
        return functools.reduce(lambda a, b: a + b, [lanes(row, t) for t in range(tiles)])

    def k_times(*vectors):
        accs = [jnp.zeros((LANES, LANES), F32) for _ in vectors]
        for t in range(tiles):
            k = kv[:, t * LANES : (t + 1) * LANES]
            accs = [a + k * lanes(v, t) for a, v in zip(accs, vectors)]
        return [as_row(a) for a in accs]

    (kv0,) = k_times(v0c)
    lane = lax.broadcasted_iota(jnp.int32, (1, LANES), 1)

    def by_two(row):
        return row + pltpu.roll(row, 64, 1)

    def by_four(row):
        row = by_two(row)
        return row + pltpu.roll(row, 32, 1)

    tp1[pr] = jnp.concatenate(
        [row_part, rhs_part, kv0,
         jnp.where(lane < 64, by_two(fold(v0c * v0c)), by_two(fold(v0c * dc * v0c)))],
        axis=0,
    )
    pl.semaphore_wait(ready, 7)
    to_proto(lambda other: (tp1.at[pr], tp1.at[pr]), 1)

    x, core = lax.div(dp, 2), lax.rem(dp, 2)
    sibling = 2 * x + 1 - core

    def block(d):
        return ef.at[pl.ds(pl.multiple_of(d * LANES, LANES), LANES)]

    for k in (2, 1, 3):
        pltpu.make_async_remote_copy(
            src_ref=ev, dst_ref=block(dp), send_sem=send.at[6], recv_sem=recv.at[6],
            device_id=(2 * lax.rem(x + k, 4) + core, pr), device_id_type=MESH,
        ).start()
    ef[mine, :] = ev[...]

    guess = col_pair[1:2] * (1.0 / rows_all) / dc
    for t in range(tiles):
        at = pl.ds(t * LANES, LANES)
        wv[:, at] = (kv[:, at] * (gv[:, at].astype(F32) - lanes(guess, t))).astype(BF16)

    def weighted_terms(to, first):
        lhs = jnp.concatenate([et[2 * j + first] for j in range(4)], axis=0)
        for c in range(cols // 512):
            at = pl.ds(c * 512, 512)
            part = jnp.dot(lhs, wv[:, at], preferred_element_type=F32).astype(BF16)
            for j in range(4):
                to[j, :, at] = part[64 * j : 64 * j + 64]

    weighted_terms(sp_out, 1 - core)
    pltpu.make_async_remote_copy(
        src_ref=sp_out, dst_ref=sp_in, send_sem=send.at[8], recv_sem=recv.at[8],
        device_id=(sibling, pr), device_id_type=MESH,
    ).start()
    weighted_terms(sp_own, core)
    for d in range(N_DP):
        erc[d * LANES : (d + 1) * LANES, :] = as_column(td1[d, 0:1, cols:])
    wait_bytes(tp1.at[pl.ds(0, N_PROTO - 1)], recv.at[1])
    one = jnp.sum(tp1[...], axis=0)
    dr = one[0:1] * (1.0 / cols_all) + RIDGE
    v0r = one[1:2] * (1.0 / root_cols)
    kv0 = one[2:3]
    s0 = total(jnp.where(lane < 64, one[3:4], 0.0))
    s1 = total(jnp.where(lane < 64, 0.0, one[3:4]))
    p_r = dr * v0r + coupling * kv0

    v0_col, p_col = as_column(v0r), as_column(p_r)
    for t in range(tiles):
        at = pl.ds(t * LANES, LANES)
        k = kv[:, at]
        td2[dp, 0:1, at] = jnp.sum(k * v0_col, axis=0, keepdims=True)
        td2[dp, 1:2, at] = jnp.sum(k * p_col, axis=0, keepdims=True)
    td2[dp, 0:1, pl.ds(cols, LANES)] = v0r * v0r
    td2[dp, 1:2, pl.ds(cols, LANES)] = v0r * (dr * v0r + (2.0 * coupling) * kv0)
    td2[dp, 0:1, pl.ds(cols + LANES, LANES)] = v0r
    td2[dp, 1:2, pl.ds(cols + LANES, LANES)] = p_r
    to_dp(td2, 2)

    def whole_kernel(c):
        at = pl.ds(c * wide, wide)
        scores = lax.dot_general(
            ef[...], pv[at, :], (((1,), (1,)), ((), ())), preferred_element_type=F32
        )
        shift = jnp.concatenate([erc[...], erc[...]], axis=1)
        kf[:, at] = jnp.exp(scores * (1.0 / TEMP) + shift + pc[:, at]).astype(BF16)

    wait_bytes(ef.at[pl.ds(0, 3 * LANES)], recv.at[6])
    for j in range(4):
        pltpu.make_async_remote_copy(
            src_ref=block(2 * j + core), dst_ref=block(2 * j + core),
            send_sem=send.at[7], recv_sem=recv.at[7],
            device_id=(sibling, pr), device_id_type=MESH,
        ).start()
    wait_bytes(sp_in, recv.at[8])
    for j in range(4):
        sp_own[j] = (sp_own[j].astype(F32) + sp_in[j].astype(F32)).astype(BF16)
    wait_bytes(td2.at[pl.ds(0, N_DP - 1)], recv.at[2])
    two = jnp.sum(td2[...], axis=0)
    m0 = s0 + total(two[0:1, cols : cols + LANES])
    m1 = s1 + total(two[1:2, cols : cols + LANES])
    theta = m1 / m0
    step = m0 / m1
    ktv0, ktp = two[0:1, :cols], two[1:2, :cols]
    r1r = v0r - step * p_r
    r1c = v0c - step * (dc * v0c + coupling * ktv0)
    ktr1 = ktv0 - step * ktp
    wc = step * (dc * r1c + coupling * ktr1) - r1c

    kr1, kw = k_times(r1c, wc)
    q = [by_four(fold(v)) for v in
         (r1c * r1c, r1c * wc, v0c * wc, wc * wc, wc * dc * wc, v0c * r1c)]
    tp2[pr] = jnp.concatenate(
        [kr1, kw,
         jnp.where(lane < 64, jnp.where(lane < 32, q[0], q[1]), jnp.where(lane < 96, q[2], q[3])),
         jnp.where(lane < 64, jnp.where(lane < 32, q[4], q[5]), 0.0)],
        axis=0,
    )
    to_proto(lambda other: (tp2.at[pr], tp2.at[pr]), 3)
    right, left, across = (lax.rem(x + k, 4) for k in (1, 3, 2))
    for i, to in enumerate((right, left)):
        pltpu.make_async_remote_copy(
            src_ref=sp_own.at[across, pl.ds(32 * i, 32)], dst_ref=s2.at[i],
            send_sem=send.at[9], recv_sem=recv.at[9],
            device_id=(2 * to + core, pr), device_id_type=MESH,
        ).start()
    wait_bytes(ef.at[pl.ds(0, 4 * LANES)], recv.at[7])
    for d in range(N_DP):
        eg[d] = ef[d * LANES : (d + 1) * LANES, pl.ds(pl.multiple_of(x * LANES, LANES), LANES)].astype(F32).T
    for c in range(cols // wide):
        whole_kernel(c)
    share = pl.ds(pl.multiple_of(64 * core, 64), 64)
    lhs = jnp.concatenate([eg[d, share, :] for d in range(N_DP)], axis=1).astype(BF16)
    for c in range(cols // 512):
        at = pl.ds(c * 512, 512)
        uf[:, at] = jnp.dot(lhs, kf[:, at], preferred_element_type=F32)
    wait_bytes(tp2.at[pl.ds(0, N_PROTO - 1)], recv.at[3])
    three = jnp.sum(tp2[...], axis=0)
    kr1, kw = three[0:1], three[1:2]
    wr = step * (dr * r1r + coupling * kr1) - r1r
    td3[dp] = jnp.concatenate(
        [r1r * r1r, r1r * wr, v0r * wr, wr * wr, wr * (dr * wr + (2.0 * coupling) * kw), v0r * r1r,
         wr, jnp.zeros((1, LANES), F32)],
        axis=0,
    )
    to_dp(td3, 4)
    wait_bytes(s2, recv.at[9])
    for i, to in enumerate((right, left)):
        half = pl.ds(32 * i, 32)
        sp_own[to, half] = (sp_own[to, half].astype(F32) + s2[i].astype(F32)).astype(BF16)
        pltpu.make_async_remote_copy(
            src_ref=sp_own.at[to], dst_ref=sx.at[i], send_sem=send.at[10], recv_sem=recv.at[10],
            device_id=(2 * to + core, pr), device_id_type=MESH,
        ).start()
    five = [
        total(jnp.where((lane >= 32 * g) & (lane < 32 * g + 32), three[r : r + 1], 0.0))
        for r, g in ((2, 0), (2, 1), (2, 2), (2, 3), (3, 0), (3, 1))
    ]
    sol_cols = [as_column(v) for v in (v0r, r1r, wr)]
    wait_bytes(td3.at[pl.ds(0, N_DP - 1)], recv.at[4])
    four = total(jnp.sum(td3[...], axis=0))
    r1r1, r1w, v0w = four[0:1] + five[0], four[1:2] + five[1], four[2:3] + five[2]
    ww, waw, v0r1 = four[3:4] + five[3], (four[4:5] + five[4]) * step, four[5:6] + five[5]
    y0, y1, y2 = solve(m0, v0r1, v0w, r1r1, r1w, ww, waw)
    y0, y1, y2 = y0 * step, y1 * step, y2 * step
    sol_c = (y0 * v0c + y1 * r1c + y2 * wc) * (1.0 / root_rows)

    ys = [v * (1.0 / root_cols) for v in (y0, y1, y2)]
    sol_col = ys[0] * sol_cols[0] + ys[1] * sol_cols[1] + ys[2] * sol_cols[2]
    for t in range(tiles):
        at = pl.ds(t * LANES, LANES)
        g = gv[:, at].astype(F32)
        wv[:, at] = (kv[:, at] * (g - sol_col - lanes(sol_c, t)) * (1.0 / TEMP)).astype(BF16)
    ge = jnp.dot(wv[...], pv[...], preferred_element_type=F32)
    for j in range(4):
        rs_out[pl.ds(16 * j, 16)] = ge[:, j * LANES : (j + 1) * LANES].T.reshape(16, 8, LANES).astype(BF16)
    to_proto(lambda other: (rs_out.at[other], rs_in.at[pr]), 5)
    rs_in[pr] = rs_out[pr]
    wait_bytes(sx, recv.at[10])
    for c in range(cols // 512):
        at = pl.ds(c * 512, 512)
        both = sx[0, :, at].astype(F32) + sx[1, :, at].astype(F32)
        sf[:, at] = sp_own[x, :, at].astype(F32) + both

    scaled = []
    for d in range(N_DP):
        v0d = td2[d, 0:1, pl.ds(cols + LANES, LANES)]
        r1d = v0d - step * td2[d, 1:2, pl.ds(cols + LANES, LANES)]
        sol_d = (y0 * v0d + y1 * r1d + y2 * td3[d, 6:7, :]) * (1.0 / root_cols)
        scaled.append((eg[d, share, :] * sol_d).astype(BF16))
    lhs = jnp.concatenate(scaled, axis=1)
    for c in range(cols // 512):
        at = pl.ds(c * 512, 512)
        terms = jnp.dot(lhs, kf[:, at], preferred_element_type=F32)
        part = sf[:, at] - terms - uf[:, at] * (sol_c - guess)[:, c * 512 : (c + 1) * 512]
        o_proto[:, at] = (part * (1.0 / TEMP)).astype(BF16)
    wait_bytes(rs_in.at[pl.ds(0, N_PROTO - 1)], recv.at[5])
    o_emb[...] = jnp.sum(rs_in[...].astype(F32), axis=0)

    wait_bytes(td1.at[pl.ds(0, N_DP - 1)], send.at[0])
    wait_bytes(tp1.at[pl.ds(0, N_PROTO - 1)], send.at[1])
    wait_bytes(td2.at[pl.ds(0, N_DP - 1)], send.at[2])
    wait_bytes(tp2.at[pl.ds(0, N_PROTO - 1)], send.at[3])
    wait_bytes(td3.at[pl.ds(0, N_DP - 1)], send.at[4])
    wait_bytes(rs_out.at[pl.ds(0, N_PROTO - 1)], send.at[5])
    wait_bytes(ef.at[pl.ds(0, 3 * LANES)], send.at[6])
    wait_bytes(ef.at[pl.ds(0, 4 * LANES)], send.at[7])
    wait_bytes(sp_out, send.at[8])
    wait_bytes(s2, send.at[9])
    wait_bytes(sx, send.at[10])


def shards(
    embeddings, prototypes, embedding_log_potential, prototype_log_potential, scaled_plan_gradient
):
    rows, width = embeddings.shape
    cols = prototypes.shape[0]
    share = width // N_DP
    any_space = pl.BlockSpec(memory_space=pl.ANY)
    vmem = pl.BlockSpec(memory_space=pltpu.VMEM)
    ge, gp = pl.pallas_call(
        functools.partial(body, rows * N_DP, cols * N_PROTO),
        out_shape=(
            jax.ShapeDtypeStruct((width // N_PROTO, rows), F32),
            jax.ShapeDtypeStruct((share, cols), BF16),
        ),
        in_specs=[any_space] * 5,
        out_specs=(vmem, vmem),
        scratch_shapes=[
            pltpu.VMEM((rows, width), BF16),
            pltpu.VMEM((N_DP, share, rows), BF16),
            pltpu.VMEM((cols, width), BF16),
            pltpu.VMEM((1, rows), F32),
            pltpu.VMEM((1, cols), F32),
            pltpu.VMEM((rows, cols), BF16),
            pltpu.VMEM((rows, cols), F32),
            pltpu.VMEM((rows, cols), BF16),
            pltpu.VMEM((N_DP, 2, cols + LANES), F32),
            pltpu.VMEM((N_DP, 2, cols + 2 * LANES), F32),
            pltpu.VMEM((N_DP, 8, LANES), F32),
            pltpu.VMEM((N_PROTO, 4, LANES), F32),
            pltpu.VMEM((N_PROTO, 4, LANES), F32),
            pltpu.VMEM((N_PROTO, 8, LANES), BF16),
            pltpu.VMEM((N_PROTO, 8, LANES), BF16),
            pltpu.VMEM((rows * N_DP, width), BF16),
            pltpu.VMEM((N_DP, LANES, rows), F32),
            pltpu.VMEM((rows * N_DP, LANES), F32),
            pltpu.VMEM((rows * N_DP, cols), BF16),
            pltpu.VMEM((share, cols), F32),
            pltpu.VMEM((share, cols), F32),
            pltpu.VMEM((4, share, cols), BF16),
            pltpu.VMEM((4, share, cols), BF16),
            pltpu.VMEM((4, share, cols), BF16),
            pltpu.VMEM((2, share // 2, cols), BF16),
            pltpu.VMEM((2, share, cols), BF16),
            pltpu.SemaphoreType.DMA((5,)),
            pltpu.SemaphoreType.REGULAR,
            pltpu.SemaphoreType.DMA((11,)),
            pltpu.SemaphoreType.DMA((11,)),
        ],
        compiler_params=pltpu.CompilerParams(
            collective_id=0, has_side_effects=True, vmem_limit_bytes=56 * 1024 * 1024
        ),
    )(
        embeddings,
        prototypes,
        embedding_log_potential.reshape(1, rows),
        prototype_log_potential.reshape(1, cols),
        scaled_plan_gradient,
    )
    return ge.T, gp.T


def solution(mesh):
    return jax.shard_map(
        shards,
        mesh=mesh,
        in_specs=(P("dp", None), P("proto", None), P("dp"), P("proto"), P("dp", "proto")),
        out_specs=(P("dp", "proto"), P("proto", "dp")),
        check_vma=False,
    )
```

```python
import functools
import math

import jax
import jax.numpy as jnp
from jax import lax
from jax.experimental import pallas as pl
from jax.experimental.pallas import tpu as pltpu
from jax.sharding import PartitionSpec as P

MESH = pl.DeviceIdType.MESH
TEMP = 0.05
RIDGE = 0.05
N_DP = 8
N_Z = 8
N_Y = 8
N_PROTO = N_Z * N_Y
LANES = 128
F32 = jnp.float32
BF16 = jnp.bfloat16


def total(values):
    return jnp.sum(values, axis=1, keepdims=True)


def as_column(row):
    return jnp.broadcast_to(row, (LANES, LANES)).T


def as_row(acc):
    return jnp.sum(acc.T, axis=0, keepdims=True)


def hops(dz, dy):
    return min(dz, N_Z - dz) + min(dy, N_Y - dy)


FAR_FIRST = sorted(
    [(dz, dy) for dz in range(N_Z) for dy in range(N_Y) if dz or dy], key=lambda o: -hops(*o)
)
DP_FAR_FIRST = (4, 5, 3, 2, 6, 1, 7)
FAR = (4, 3, 5, 2, 6, 1, 7)


def wait_bytes(ref, sem):
    pltpu.make_async_copy(ref, ref, sem).wait()


def solve(m0, b1, b2, r1r1, r1w, ww, waw):
    g00, g01, g02 = m0, b1 - r1r1, b2 - r1w
    g11, g12, g22 = r1w + r1r1, ww + r1w, waw
    l10, l20 = g01 / g00, g02 / g00
    d1 = g11 - g01 * l10
    i1 = jnp.where(d1 > 1e-6 * g11, 1.0 / d1, 0.0)
    t = g12 - l20 * g01
    l21 = t * i1
    d2 = g22 - l20 * g02 - l21 * t
    i2 = jnp.where(d2 > 1e-6 * g22, 1.0 / d2, 0.0)
    z1 = b1 - l10 * m0
    z2 = b2 - l20 * m0 - l21 * z1
    y2 = z2 * i2
    y1 = z1 * i1 - l21 * y2
    y0 = 1.0 - l10 * y1 - l20 * y2
    return y0, y1, y2


def body(
    rows_all, cols_all,
    e_hbm, p_hbm, er_hbm, pc_hbm, g_hbm, o_emb, o_proto,
    ev, et, pv, er, pc, gv, kv, wv, td1, td2, td3, tp1, tp2, rs_out, rs_in,
    ef, eg, erc, kf, uf, sf, sp_out, sp_own, sp_in, s2, sx,
    op, hs, in_sem, send, recv,
):
    dp, pr = lax.axis_index("dp"), lax.axis_index("proto")
    z, y = lax.div(pr, N_Y), lax.rem(pr, N_Y)
    cols = pv.shape[0]
    tiles = cols // LANES
    root_cols = math.sqrt(cols_all)
    root_rows = math.sqrt(rows_all)
    coupling = 1.0 / (root_rows * root_cols)

    loads = [
        pltpu.make_async_copy(src, dst, in_sem.at[i])
        for i, (src, dst) in enumerate(
            [(e_hbm, ev), (p_hbm, pv), (er_hbm, er), (pc_hbm, pc), (g_hbm, gv)]
        )
    ]
    for load in loads:
        load.start()

    barrier = pltpu.get_barrier_semaphore()
    for k in FAR:
        pl.semaphore_signal(
            barrier, inc=1, device_id=(dp, z * N_Y + lax.rem(y + k, N_Y)), device_id_type=MESH
        )
        pl.semaphore_signal(
            barrier, inc=1, device_id=(dp, lax.rem(z + k, N_Z) * N_Y + y), device_id_type=MESH
        )
    for k in DP_FAR_FIRST:
        pl.semaphore_signal(
            barrier, inc=1, device_id=(lax.rem(dp + k, N_DP), pr), device_id_type=MESH
        )
    for load in loads:
        load.wait()

    def to_dp(buf, i):
        for k in DP_FAR_FIRST:
            pltpu.make_async_remote_copy(
                src_ref=buf.at[dp], dst_ref=buf.at[dp], send_sem=send.at[i], recv_sem=recv.at[i],
                device_id=(lax.rem(dp + k, N_DP), pr), device_id_type=MESH,
            ).start()

    def to_proto(make, i):
        for dz, dy in FAR_FIRST:
            other = lax.rem(z + dz, N_Z) * N_Y + lax.rem(y + dy, N_Y)
            src, dst = make(other)
            pltpu.make_async_remote_copy(
                src_ref=src, dst_ref=dst, send_sem=send.at[i], recv_sem=recv.at[i],
                device_id=(dp, other), device_id_type=MESH,
            ).start()

    hs[z] = jnp.zeros((8, LANES), F32)
    er_col = as_column(er[...])
    row_acc = jnp.zeros((LANES, LANES), F32)
    rhs_acc = jnp.zeros((LANES, LANES), F32)
    wide = 256
    er_wide = jnp.concatenate([er_col, er_col], axis=1)
    for c in range(cols // wide):
        at = pl.ds(c * wide, wide)
        scores = lax.dot_general(
            ev[...], pv[at, :], (((1,), (1,)), ((), ())), preferred_element_type=F32
        )
        k = jnp.exp(scores * (1.0 / TEMP) + er_wide + pc[:, at])
        kv[:, at] = k
        w = gv[:, at].astype(F32) * k
        td1[dp, 0:1, at] = jnp.sum(k, axis=0, keepdims=True)
        td1[dp, 1:2, at] = jnp.sum(w, axis=0, keepdims=True)
        row_acc += k[:, :LANES] + k[:, LANES:]
        rhs_acc += w[:, :LANES] + w[:, LANES:]
    td1[dp, 0:1, pl.ds(cols, LANES)] = er[...]
    td1[dp, 1:2, pl.ds(cols, LANES)] = er[...]
    mine = pl.ds(pl.multiple_of(dp * LANES, LANES), LANES)

    pl.semaphore_wait(barrier, 21)
    to_dp(td1, 0)
    for k in FAR:
        pltpu.make_async_remote_copy(
            src_ref=hs.at[z], dst_ref=hs.at[z], send_sem=send.at[11], recv_sem=recv.at[11],
            device_id=(dp, lax.rem(z + k, N_Z) * N_Y + y), device_id_type=MESH,
        ).start()
    row_part = as_row(row_acc)
    rhs_part = as_row(rhs_acc)

    for j in range(N_DP // 2):
        pair = ev[:, j * LANES : (j + 1) * LANES].astype(F32).T.astype(BF16)
        et[2 * j] = pair[:64]
        et[2 * j + 1] = pair[64:]
    wait_bytes(td1.at[pl.ds(0, N_DP - 1)], recv.at[0])
    col_pair = jnp.sum(td1[:, :, pl.ds(0, cols)], axis=0)
    dc = col_pair[0:1] * (1.0 / rows_all) + RIDGE
    v0c = col_pair[1:2] * (1.0 / root_rows)

    def lanes(row, t):
        return row[:, t * LANES : (t + 1) * LANES]

    def fold(row):
        return functools.reduce(lambda a, b: a + b, [lanes(row, t) for t in range(tiles)])

    def k_times(*vectors):
        accs = [jnp.zeros((LANES, LANES), F32) for _ in vectors]
        for t in range(tiles):
            k = kv[:, t * LANES : (t + 1) * LANES]
            accs = [a + k * lanes(v, t) for a, v in zip(accs, vectors)]
        return [as_row(a) for a in accs]

    (kv0,) = k_times(v0c)
    lane = lax.broadcasted_iota(jnp.int32, (1, LANES), 1)

    def by_two(row):
        return row + pltpu.roll(row, 64, 1)

    def by_four(row):
        row = by_two(row)
        return row + pltpu.roll(row, 32, 1)

    tp1[pr] = jnp.concatenate(
        [row_part, rhs_part, kv0,
         jnp.where(lane < 64, by_two(fold(v0c * v0c)), by_two(fold(v0c * dc * v0c)))],
        axis=0,
    )
    wait_bytes(hs.at[pl.ds(0, N_Z - 1)], recv.at[11])
    to_proto(lambda other: (tp1.at[pr], tp1.at[pr]), 1)

    x, core = lax.div(dp, 2), lax.rem(dp, 2)
    sibling = 2 * x + 1 - core

    def block(d):
        return ef.at[pl.ds(pl.multiple_of(d * LANES, LANES), LANES)]

    for k in (2, 1, 3):
        pltpu.make_async_remote_copy(
            src_ref=ev, dst_ref=block(dp), send_sem=send.at[6], recv_sem=recv.at[6],
            device_id=(2 * lax.rem(x + k, 4) + core, pr), device_id_type=MESH,
        ).start()
    ef[mine, :] = ev[...]

    guess = col_pair[1:2] * (1.0 / rows_all) / dc
    for t in range(tiles):
        at = pl.ds(t * LANES, LANES)
        wv[:, at] = (kv[:, at] * (gv[:, at].astype(F32) - lanes(guess, t))).astype(BF16)

    def weighted_terms(to, first):
        lhs = jnp.concatenate([et[2 * j + first] for j in range(4)], axis=0)
        for c in range(cols // 512):
            at = pl.ds(c * 512, 512)
            part = jnp.dot(lhs, wv[:, at], preferred_element_type=F32).astype(BF16)
            for j in range(4):
                to[j, :, at] = part[64 * j : 64 * j + 64]

    weighted_terms(sp_out, 1 - core)
    pltpu.make_async_remote_copy(
        src_ref=sp_out, dst_ref=sp_in, send_sem=send.at[8], recv_sem=recv.at[8],
        device_id=(sibling, pr), device_id_type=MESH,
    ).start()
    weighted_terms(sp_own, core)
    for d in range(N_DP):
        erc[d * LANES : (d + 1) * LANES, :] = as_column(td1[d, 0:1, cols:])
    wait_bytes(tp1.at[pl.ds(0, N_PROTO - 1)], recv.at[1])
    one = jnp.sum(tp1[...], axis=0)
    dr = one[0:1] * (1.0 / cols_all) + RIDGE
    v0r = one[1:2] * (1.0 / root_cols)
    kv0 = one[2:3]
    s0 = total(jnp.where(lane < 64, one[3:4], 0.0))
    s1 = total(jnp.where(lane < 64, 0.0, one[3:4]))
    p_r = dr * v0r + coupling * kv0

    v0_col, p_col = as_column(v0r), as_column(p_r)
    for t in range(tiles):
        at = pl.ds(t * LANES, LANES)
        k = kv[:, at]
        td2[dp, 0:1, at] = jnp.sum(k * v0_col, axis=0, keepdims=True)
        td2[dp, 1:2, at] = jnp.sum(k * p_col, axis=0, keepdims=True)
    td2[dp, 0:1, pl.ds(cols, LANES)] = v0r * v0r
    td2[dp, 1:2, pl.ds(cols, LANES)] = v0r * (dr * v0r + (2.0 * coupling) * kv0)
    td2[dp, 0:1, pl.ds(cols + LANES, LANES)] = v0r
    td2[dp, 1:2, pl.ds(cols + LANES, LANES)] = p_r
    to_dp(td2, 2)

    def whole_kernel(c):
        at = pl.ds(c * wide, wide)
        scores = lax.dot_general(
            ef[...], pv[at, :], (((1,), (1,)), ((), ())), preferred_element_type=F32
        )
        shift = jnp.concatenate([erc[...], erc[...]], axis=1)
        kf[:, at] = jnp.exp(scores * (1.0 / TEMP) + shift + pc[:, at]).astype(BF16)

    wait_bytes(ef.at[pl.ds(0, 3 * LANES)], recv.at[6])
    for j in range(4):
        pltpu.make_async_remote_copy(
            src_ref=block(2 * j + core), dst_ref=block(2 * j + core),
            send_sem=send.at[7], recv_sem=recv.at[7],
            device_id=(sibling, pr), device_id_type=MESH,
        ).start()
    wait_bytes(sp_in, recv.at[8])
    for j in range(4):
        sp_own[j] = (sp_own[j].astype(F32) + sp_in[j].astype(F32)).astype(BF16)
    wait_bytes(td2.at[pl.ds(0, N_DP - 1)], recv.at[2])
    two = jnp.sum(td2[...], axis=0)
    m0 = s0 + total(two[0:1, cols : cols + LANES])
    m1 = s1 + total(two[1:2, cols : cols + LANES])
    theta = m1 / m0
    step = m0 / m1
    ktv0, ktp = two[0:1, :cols], two[1:2, :cols]
    r1r = v0r - step * p_r
    r1c = v0c - step * (dc * v0c + coupling * ktv0)
    ktr1 = ktv0 - step * ktp
    wc = step * (dc * r1c + coupling * ktr1) - r1c

    kr1, kw = k_times(r1c, wc)
    q = [by_four(fold(v)) for v in
         (r1c * r1c, r1c * wc, v0c * wc, wc * wc, wc * dc * wc, v0c * r1c)]
    tp2[pr] = jnp.concatenate(
        [kr1, kw,
         jnp.where(lane < 64, jnp.where(lane < 32, q[0], q[1]), jnp.where(lane < 96, q[2], q[3])),
         jnp.where(lane < 64, jnp.where(lane < 32, q[4], q[5]), 0.0)],
        axis=0,
    )
    to_proto(lambda other: (tp2.at[pr], tp2.at[pr]), 3)
    right, left, across = (lax.rem(x + k, 4) for k in (1, 3, 2))
    for i, to in enumerate((right, left)):
        pltpu.make_async_remote_copy(
            src_ref=sp_own.at[across, pl.ds(32 * i, 32)], dst_ref=s2.at[i],
            send_sem=send.at[9], recv_sem=recv.at[9],
            device_id=(2 * to + core, pr), device_id_type=MESH,
        ).start()
    wait_bytes(ef.at[pl.ds(0, 4 * LANES)], recv.at[7])
    for d in range(N_DP):
        eg[d] = ef[d * LANES : (d + 1) * LANES, pl.ds(pl.multiple_of(x * LANES, LANES), LANES)].astype(F32).T
    for c in range(cols // wide):
        whole_kernel(c)
    share = pl.ds(pl.multiple_of(64 * core, 64), 64)
    lhs = jnp.concatenate([eg[d, share, :] for d in range(N_DP)], axis=1).astype(BF16)
    for c in range(cols // 512):
        at = pl.ds(c * 512, 512)
        uf[:, at] = jnp.dot(lhs, kf[:, at], preferred_element_type=F32)
    wait_bytes(tp2.at[pl.ds(0, N_PROTO - 1)], recv.at[3])
    three = jnp.sum(tp2[...], axis=0)
    kr1, kw = three[0:1], three[1:2]
    wr = step * (dr * r1r + coupling * kr1) - r1r
    td3[dp] = jnp.concatenate(
        [r1r * r1r, r1r * wr, v0r * wr, wr * wr, wr * (dr * wr + (2.0 * coupling) * kw), v0r * r1r,
         wr, jnp.zeros((1, LANES), F32)],
        axis=0,
    )
    to_dp(td3, 4)
    wait_bytes(s2, recv.at[9])
    for i, to in enumerate((right, left)):
        half = pl.ds(32 * i, 32)
        sp_own[to, half] = (sp_own[to, half].astype(F32) + s2[i].astype(F32)).astype(BF16)
        pltpu.make_async_remote_copy(
            src_ref=sp_own.at[to], dst_ref=sx.at[i], send_sem=send.at[10], recv_sem=recv.at[10],
            device_id=(2 * to + core, pr), device_id_type=MESH,
        ).start()
    five = [
        total(jnp.where((lane >= 32 * g) & (lane < 32 * g + 32), three[r : r + 1], 0.0))
        for r, g in ((2, 0), (2, 1), (2, 2), (2, 3), (3, 0), (3, 1))
    ]
    sol_cols = [as_column(v) for v in (v0r, r1r, wr)]
    wait_bytes(td3.at[pl.ds(0, N_DP - 1)], recv.at[4])
    four = total(jnp.sum(td3[...], axis=0))
    r1r1, r1w, v0w = four[0:1] + five[0], four[1:2] + five[1], four[2:3] + five[2]
    ww, waw, v0r1 = four[3:4] + five[3], (four[4:5] + five[4]) * step, four[5:6] + five[5]
    y0, y1, y2 = solve(m0, v0r1, v0w, r1r1, r1w, ww, waw)
    y0, y1, y2 = y0 * step, y1 * step, y2 * step
    sol_c = (y0 * v0c + y1 * r1c + y2 * wc) * (1.0 / root_rows)

    ys = [v * (1.0 / root_cols) for v in (y0, y1, y2)]
    sol_col = ys[0] * sol_cols[0] + ys[1] * sol_cols[1] + ys[2] * sol_cols[2]
    for t in range(tiles):
        at = pl.ds(t * LANES, LANES)
        g = gv[:, at].astype(F32)
        wv[:, at] = (kv[:, at] * (g - sol_col - lanes(sol_c, t)) * (1.0 / TEMP)).astype(BF16)
    ge = jnp.dot(wv[...], pv[...], preferred_element_type=F32)
    for j in range(4):
        rs_out[pl.ds(16 * j, 16)] = ge[:, j * LANES : (j + 1) * LANES].T.reshape(16, 8, LANES).astype(BF16)
    to_proto(lambda other: (rs_out.at[other], rs_in.at[pr]), 5)
    rs_in[pr] = rs_out[pr]
    wait_bytes(sx, recv.at[10])
    for c in range(cols // 512):
        at = pl.ds(c * 512, 512)
        both = sx[0, :, at].astype(F32) + sx[1, :, at].astype(F32)
        sf[:, at] = sp_own[x, :, at].astype(F32) + both

    scaled = []
    for d in range(N_DP):
        v0d = td2[d, 0:1, pl.ds(cols + LANES, LANES)]
        r1d = v0d - step * td2[d, 1:2, pl.ds(cols + LANES, LANES)]
        sol_d = (y0 * v0d + y1 * r1d + y2 * td3[d, 6:7, :]) * (1.0 / root_cols)
        scaled.append((eg[d, share, :] * sol_d).astype(BF16))
    lhs = jnp.concatenate(scaled, axis=1)
    for c in range(cols // 512):
        at = pl.ds(c * 512, 512)
        terms = jnp.dot(lhs, kf[:, at], preferred_element_type=F32)
        part = sf[:, at] - terms - uf[:, at] * (sol_c - guess)[:, c * 512 : (c + 1) * 512]
        op[:, at] = (part * (1.0 / TEMP)).astype(BF16)
    store = pltpu.make_async_copy(op, o_proto, in_sem.at[5])
    store.start()
    wait_bytes(rs_in.at[pl.ds(0, N_PROTO - 1)], recv.at[5])
    o_emb[...] = jnp.sum(rs_in[...].astype(F32), axis=0)

    store.wait()
    wait_bytes(hs.at[pl.ds(0, N_Z - 1)], send.at[11])
    wait_bytes(td1.at[pl.ds(0, N_DP - 1)], send.at[0])
    wait_bytes(tp1.at[pl.ds(0, N_PROTO - 1)], send.at[1])
    wait_bytes(td2.at[pl.ds(0, N_DP - 1)], send.at[2])
    wait_bytes(tp2.at[pl.ds(0, N_PROTO - 1)], send.at[3])
    wait_bytes(td3.at[pl.ds(0, N_DP - 1)], send.at[4])
    wait_bytes(rs_out.at[pl.ds(0, N_PROTO - 1)], send.at[5])
    wait_bytes(ef.at[pl.ds(0, 3 * LANES)], send.at[6])
    wait_bytes(ef.at[pl.ds(0, 4 * LANES)], send.at[7])
    wait_bytes(sp_out, send.at[8])
    wait_bytes(s2, send.at[9])
    wait_bytes(sx, send.at[10])


def shards(
    embeddings, prototypes, embedding_log_potential, prototype_log_potential, scaled_plan_gradient
):
    rows, width = embeddings.shape
    cols = prototypes.shape[0]
    share = width // N_DP
    any_space = pl.BlockSpec(memory_space=pl.ANY)
    vmem = pl.BlockSpec(memory_space=pltpu.VMEM)
    ge, gp = pl.pallas_call(
        functools.partial(body, rows * N_DP, cols * N_PROTO),
        out_shape=(
            jax.ShapeDtypeStruct((width // N_PROTO, rows), F32),
            jax.ShapeDtypeStruct((share, cols), BF16),
        ),
        in_specs=[any_space] * 5,
        out_specs=(vmem, any_space),
        scratch_shapes=[
            pltpu.VMEM((rows, width), BF16),
            pltpu.VMEM((N_DP, share, rows), BF16),
            pltpu.VMEM((cols, width), BF16),
            pltpu.VMEM((1, rows), F32),
            pltpu.VMEM((1, cols), F32),
            pltpu.VMEM((rows, cols), BF16),
            pltpu.VMEM((rows, cols), F32),
            pltpu.VMEM((rows, cols), BF16),
            pltpu.VMEM((N_DP, 2, cols + LANES), F32),
            pltpu.VMEM((N_DP, 2, cols + 2 * LANES), F32),
            pltpu.VMEM((N_DP, 8, LANES), F32),
            pltpu.VMEM((N_PROTO, 4, LANES), F32),
            pltpu.VMEM((N_PROTO, 4, LANES), F32),
            pltpu.VMEM((N_PROTO, 8, LANES), BF16),
            pltpu.VMEM((N_PROTO, 8, LANES), BF16),
            pltpu.VMEM((rows * N_DP, width), BF16),
            pltpu.VMEM((N_DP, LANES, rows), F32),
            pltpu.VMEM((rows * N_DP, LANES), F32),
            pltpu.VMEM((rows * N_DP, cols), BF16),
            pltpu.VMEM((share, cols), F32),
            pltpu.VMEM((share, cols), F32),
            pltpu.VMEM((4, share, cols), BF16),
            pltpu.VMEM((4, share, cols), BF16),
            pltpu.VMEM((4, share, cols), BF16),
            pltpu.VMEM((2, share // 2, cols), BF16),
            pltpu.VMEM((2, share, cols), BF16),
            pltpu.VMEM((share, cols), BF16),
            pltpu.VMEM((N_Z, 8, LANES), F32),
            pltpu.SemaphoreType.DMA((6,)),
            pltpu.SemaphoreType.DMA((12,)),
            pltpu.SemaphoreType.DMA((12,)),
        ],
        compiler_params=pltpu.CompilerParams(
            collective_id=0, has_side_effects=True, vmem_limit_bytes=56 * 1024 * 1024
        ),
    )(
        embeddings,
        prototypes,
        embedding_log_potential.reshape(1, rows),
        prototype_log_potential.reshape(1, cols),
        scaled_plan_gradient,
    )
    return ge.T, gp.T


def solution(mesh):
    return jax.shard_map(
        shards,
        mesh=mesh,
        in_specs=(P("dp", None), P("proto", None), P("dp"), P("proto"), P("dp", "proto")),
        out_specs=(P("dp", "proto"), P("proto", "dp")),
        check_vma=False,
    )
```

```python
import functools
import math

import jax
import jax.numpy as jnp
from jax import lax
from jax.experimental import pallas as pl
from jax.experimental.pallas import tpu as pltpu
from jax.sharding import PartitionSpec as P

MESH = pl.DeviceIdType.MESH
TEMP = 0.05
RIDGE = 0.05
N_DP = 8
N_Z = 8
N_Y = 8
N_PROTO = N_Z * N_Y
LANES = 128
F32 = jnp.float32
BF16 = jnp.bfloat16


def total(values):
    return jnp.sum(values, axis=1, keepdims=True)


def as_column(row):
    return jnp.broadcast_to(row, (LANES, LANES)).T


def as_row(acc):
    return jnp.sum(acc.T, axis=0, keepdims=True)


def hops(dz, dy):
    return min(dz, N_Z - dz) + min(dy, N_Y - dy)


FAR_FIRST = sorted(
    [(dz, dy) for dz in range(N_Z) for dy in range(N_Y) if dz or dy], key=lambda o: -hops(*o)
)
DP_FAR_FIRST = (4, 5, 3, 2, 6, 1, 7)
FAR = (4, 3, 5, 2, 6, 1, 7)


def wait_bytes(ref, sem):
    pltpu.make_async_copy(ref, ref, sem).wait()


def solve(m0, b1, b2, r1r1, r1w, ww, waw):
    g00, g01, g02 = m0, b1 - r1r1, b2 - r1w
    g11, g12, g22 = r1w + r1r1, ww + r1w, waw
    l10, l20 = g01 / g00, g02 / g00
    d1 = g11 - g01 * l10
    i1 = jnp.where(d1 > 1e-6 * g11, 1.0 / d1, 0.0)
    t = g12 - l20 * g01
    l21 = t * i1
    d2 = g22 - l20 * g02 - l21 * t
    i2 = jnp.where(d2 > 1e-6 * g22, 1.0 / d2, 0.0)
    z1 = b1 - l10 * m0
    z2 = b2 - l20 * m0 - l21 * z1
    y2 = z2 * i2
    y1 = z1 * i1 - l21 * y2
    y0 = 1.0 - l10 * y1 - l20 * y2
    return y0, y1, y2


def body(
    rows_all, cols_all,
    e_hbm, p_hbm, er_hbm, pc_hbm, g_hbm, o_emb, o_proto,
    ev, et, pv, er, pc, gv, kv, wv, td1, td2, td3, tp1, tp2, rs_out, rs_in,
    ef, eg, erc, kf, uf, sf, sp_out, sp_own, sp_in, s2, sx,
    op, hs, in_sem, send, recv,
):
    dp, pr = lax.axis_index("dp"), lax.axis_index("proto")
    z, y = lax.div(pr, N_Y), lax.rem(pr, N_Y)
    cols = pv.shape[0]
    tiles = cols // LANES
    root_cols = math.sqrt(cols_all)
    root_rows = math.sqrt(rows_all)
    coupling = 1.0 / (root_rows * root_cols)

    loads = [
        pltpu.make_async_copy(src, dst, in_sem.at[i])
        for i, (src, dst) in enumerate(
            [(e_hbm, ev), (p_hbm, pv), (er_hbm, er), (pc_hbm, pc), (g_hbm, gv)]
        )
    ]
    for load in loads:
        load.start()

    barrier = pltpu.get_barrier_semaphore()
    for k in FAR:
        pl.semaphore_signal(
            barrier, inc=1, device_id=(dp, z * N_Y + lax.rem(y + k, N_Y)), device_id_type=MESH
        )
        pl.semaphore_signal(
            barrier, inc=1, device_id=(dp, lax.rem(z + k, N_Z) * N_Y + y), device_id_type=MESH
        )
    for k in DP_FAR_FIRST:
        pl.semaphore_signal(
            barrier, inc=1, device_id=(lax.rem(dp + k, N_DP), pr), device_id_type=MESH
        )
    for load in loads:
        load.wait()

    def to_dp(buf, i):
        for k in DP_FAR_FIRST:
            pltpu.make_async_remote_copy(
                src_ref=buf.at[dp], dst_ref=buf.at[dp], send_sem=send.at[i], recv_sem=recv.at[i],
                device_id=(lax.rem(dp + k, N_DP), pr), device_id_type=MESH,
            ).start()

    def to_proto(make, i):
        for dz, dy in FAR_FIRST:
            other = lax.rem(z + dz, N_Z) * N_Y + lax.rem(y + dy, N_Y)
            src, dst = make(other)
            pltpu.make_async_remote_copy(
                src_ref=src, dst_ref=dst, send_sem=send.at[i], recv_sem=recv.at[i],
                device_id=(dp, other), device_id_type=MESH,
            ).start()

    hs[z] = jnp.zeros((8, LANES), F32)
    er_col = as_column(er[...])
    row_acc = jnp.zeros((LANES, LANES), F32)
    rhs_acc = jnp.zeros((LANES, LANES), F32)
    wide = 256
    er_wide = jnp.concatenate([er_col, er_col], axis=1)
    for c in range(cols // wide):
        at = pl.ds(c * wide, wide)
        scores = lax.dot_general(
            ev[...], pv[at, :], (((1,), (1,)), ((), ())), preferred_element_type=F32
        )
        k = jnp.exp(scores * (1.0 / TEMP) + er_wide + pc[:, at])
        kv[:, at] = k
        w = gv[:, at].astype(F32) * k
        td1[dp, 0:1, at] = jnp.sum(k, axis=0, keepdims=True)
        td1[dp, 1:2, at] = jnp.sum(w, axis=0, keepdims=True)
        row_acc += k[:, :LANES] + k[:, LANES:]
        rhs_acc += w[:, :LANES] + w[:, LANES:]
    td1[dp, 0:1, pl.ds(cols, LANES)] = er[...]
    td1[dp, 1:2, pl.ds(cols, LANES)] = er[...]
    mine = pl.ds(pl.multiple_of(dp * LANES, LANES), LANES)

    pl.semaphore_wait(barrier, 21)
    to_dp(td1, 0)
    for k in FAR:
        pltpu.make_async_remote_copy(
            src_ref=hs.at[z], dst_ref=hs.at[z], send_sem=send.at[11], recv_sem=recv.at[11],
            device_id=(dp, lax.rem(z + k, N_Z) * N_Y + y), device_id_type=MESH,
        ).start()
    row_part = as_row(row_acc)
    rhs_part = as_row(rhs_acc)

    for j in range(N_DP // 2):
        pair = ev[:, j * LANES : (j + 1) * LANES].astype(F32).T.astype(BF16)
        et[2 * j] = pair[:64]
        et[2 * j + 1] = pair[64:]
    wait_bytes(td1.at[pl.ds(0, N_DP - 1)], recv.at[0])
    col_pair = jnp.sum(td1[:, :, pl.ds(0, cols)], axis=0)
    dc = col_pair[0:1] * (1.0 / rows_all) + RIDGE
    v0c = col_pair[1:2] * (1.0 / root_rows)

    def lanes(row, t):
        return row[:, t * LANES : (t + 1) * LANES]

    def fold(row):
        return functools.reduce(lambda a, b: a + b, [lanes(row, t) for t in range(tiles)])

    def k_times(*vectors):
        accs = [jnp.zeros((LANES, LANES), F32) for _ in vectors]
        for t in range(tiles):
            k = kv[:, t * LANES : (t + 1) * LANES]
            accs = [a + k * lanes(v, t) for a, v in zip(accs, vectors)]
        return [as_row(a) for a in accs]

    (kv0,) = k_times(v0c)
    lane = lax.broadcasted_iota(jnp.int32, (1, LANES), 1)

    def by_two(row):
        return row + pltpu.roll(row, 64, 1)

    def by_four(row):
        row = by_two(row)
        return row + pltpu.roll(row, 32, 1)

    tp1[pr] = jnp.concatenate(
        [row_part, rhs_part, kv0,
         jnp.where(lane < 64, by_two(fold(v0c * v0c)), by_two(fold(v0c * dc * v0c)))],
        axis=0,
    )
    wait_bytes(hs.at[pl.ds(0, N_Z - 1)], recv.at[11])
    to_proto(lambda other: (tp1.at[pr], tp1.at[pr]), 1)

    x, core = lax.div(dp, 2), lax.rem(dp, 2)
    sibling = 2 * x + 1 - core

    def block(d):
        return ef.at[pl.ds(pl.multiple_of(d * LANES, LANES), LANES)]

    for k in (2, 1, 3):
        pltpu.make_async_remote_copy(
            src_ref=ev, dst_ref=block(dp), send_sem=send.at[6], recv_sem=recv.at[6],
            device_id=(2 * lax.rem(x + k, 4) + core, pr), device_id_type=MESH,
        ).start()
    ef[mine, :] = ev[...]

    guess = col_pair[1:2] * (1.0 / rows_all) / dc
    for t in range(tiles):
        at = pl.ds(t * LANES, LANES)
        wv[:, at] = (kv[:, at] * (gv[:, at].astype(F32) - lanes(guess, t))).astype(BF16)

    def weighted_terms(to, first):
        lhs = jnp.concatenate([et[2 * j + first] for j in range(4)], axis=0)
        @pl.loop(0, cols // 512)
        def _(c):
            at = pl.ds(pl.multiple_of(c * 512, 512), 512)
            part = jnp.dot(lhs, wv[:, at], preferred_element_type=F32).astype(BF16)
            for j in range(4):
                to[j, :, at] = part[64 * j : 64 * j + 64]

    weighted_terms(sp_out, 1 - core)
    pltpu.make_async_remote_copy(
        src_ref=sp_out, dst_ref=sp_in, send_sem=send.at[8], recv_sem=recv.at[8],
        device_id=(sibling, pr), device_id_type=MESH,
    ).start()
    weighted_terms(sp_own, core)
    for d in range(N_DP):
        erc[d * LANES : (d + 1) * LANES, :] = as_column(td1[d, 0:1, cols:])
    wait_bytes(tp1.at[pl.ds(0, N_PROTO - 1)], recv.at[1])
    one = jnp.sum(tp1[...], axis=0)
    dr = one[0:1] * (1.0 / cols_all) + RIDGE
    v0r = one[1:2] * (1.0 / root_cols)
    kv0 = one[2:3]
    s0 = total(jnp.where(lane < 64, one[3:4], 0.0))
    s1 = total(jnp.where(lane < 64, 0.0, one[3:4]))
    p_r = dr * v0r + coupling * kv0

    v0_col, p_col = as_column(v0r), as_column(p_r)
    for t in range(tiles):
        at = pl.ds(t * LANES, LANES)
        k = kv[:, at]
        td2[dp, 0:1, at] = jnp.sum(k * v0_col, axis=0, keepdims=True)
        td2[dp, 1:2, at] = jnp.sum(k * p_col, axis=0, keepdims=True)
    td2[dp, 0:1, pl.ds(cols, LANES)] = v0r * v0r
    td2[dp, 1:2, pl.ds(cols, LANES)] = v0r * (dr * v0r + (2.0 * coupling) * kv0)
    td2[dp, 0:1, pl.ds(cols + LANES, LANES)] = v0r
    td2[dp, 1:2, pl.ds(cols + LANES, LANES)] = p_r
    to_dp(td2, 2)

    def whole_kernel(c):
        at = pl.ds(pl.multiple_of(c * wide, wide), wide)
        scores = lax.dot_general(
            ef[...], pv[at, :], (((1,), (1,)), ((), ())), preferred_element_type=F32
        )
        shift = jnp.concatenate([erc[...], erc[...]], axis=1)
        kf[:, at] = jnp.exp(scores * (1.0 / TEMP) + shift + pc[:, at]).astype(BF16)

    wait_bytes(ef.at[pl.ds(0, 3 * LANES)], recv.at[6])
    for j in range(4):
        pltpu.make_async_remote_copy(
            src_ref=block(2 * j + core), dst_ref=block(2 * j + core),
            send_sem=send.at[7], recv_sem=recv.at[7],
            device_id=(sibling, pr), device_id_type=MESH,
        ).start()
    wait_bytes(sp_in, recv.at[8])
    for j in range(4):
        sp_own[j] = (sp_own[j].astype(F32) + sp_in[j].astype(F32)).astype(BF16)
    wait_bytes(td2.at[pl.ds(0, N_DP - 1)], recv.at[2])
    two = jnp.sum(td2[...], axis=0)
    m0 = s0 + total(two[0:1, cols : cols + LANES])
    m1 = s1 + total(two[1:2, cols : cols + LANES])
    theta = m1 / m0
    step = m0 / m1
    ktv0, ktp = two[0:1, :cols], two[1:2, :cols]
    r1r = v0r - step * p_r
    r1c = v0c - step * (dc * v0c + coupling * ktv0)
    ktr1 = ktv0 - step * ktp
    wc = step * (dc * r1c + coupling * ktr1) - r1c

    kr1, kw = k_times(r1c, wc)
    q = [by_four(fold(v)) for v in
         (r1c * r1c, r1c * wc, v0c * wc, wc * wc, wc * dc * wc, v0c * r1c)]
    tp2[pr] = jnp.concatenate(
        [kr1, kw,
         jnp.where(lane < 64, jnp.where(lane < 32, q[0], q[1]), jnp.where(lane < 96, q[2], q[3])),
         jnp.where(lane < 64, jnp.where(lane < 32, q[4], q[5]), 0.0)],
        axis=0,
    )
    to_proto(lambda other: (tp2.at[pr], tp2.at[pr]), 3)
    right, left, across = (lax.rem(x + k, 4) for k in (1, 3, 2))
    for i, to in enumerate((right, left)):
        pltpu.make_async_remote_copy(
            src_ref=sp_own.at[across, pl.ds(32 * i, 32)], dst_ref=s2.at[i],
            send_sem=send.at[9], recv_sem=recv.at[9],
            device_id=(2 * to + core, pr), device_id_type=MESH,
        ).start()
    wait_bytes(ef.at[pl.ds(0, 4 * LANES)], recv.at[7])
    for d in range(N_DP):
        eg[d] = ef[d * LANES : (d + 1) * LANES, pl.ds(pl.multiple_of(x * LANES, LANES), LANES)].astype(F32).T
    pl.loop(0, cols // wide)(whole_kernel)
    share = pl.ds(pl.multiple_of(64 * core, 64), 64)
    lhs = jnp.concatenate([eg[d, share, :] for d in range(N_DP)], axis=1).astype(BF16)
    @pl.loop(0, cols // 512)
    def _(c):
        at = pl.ds(pl.multiple_of(c * 512, 512), 512)
        uf[:, at] = jnp.dot(lhs, kf[:, at], preferred_element_type=F32)
    wait_bytes(tp2.at[pl.ds(0, N_PROTO - 1)], recv.at[3])
    three = jnp.sum(tp2[...], axis=0)
    kr1, kw = three[0:1], three[1:2]
    wr = step * (dr * r1r + coupling * kr1) - r1r
    td3[dp] = jnp.concatenate(
        [r1r * r1r, r1r * wr, v0r * wr, wr * wr, wr * (dr * wr + (2.0 * coupling) * kw), v0r * r1r,
         wr, jnp.zeros((1, LANES), F32)],
        axis=0,
    )
    to_dp(td3, 4)
    wait_bytes(s2, recv.at[9])
    for i, to in enumerate((right, left)):
        half = pl.ds(32 * i, 32)
        sp_own[to, half] = (sp_own[to, half].astype(F32) + s2[i].astype(F32)).astype(BF16)
        pltpu.make_async_remote_copy(
            src_ref=sp_own.at[to], dst_ref=sx.at[i], send_sem=send.at[10], recv_sem=recv.at[10],
            device_id=(2 * to + core, pr), device_id_type=MESH,
        ).start()
    five = [
        total(jnp.where((lane >= 32 * g) & (lane < 32 * g + 32), three[r : r + 1], 0.0))
        for r, g in ((2, 0), (2, 1), (2, 2), (2, 3), (3, 0), (3, 1))
    ]
    sol_cols = [as_column(v) for v in (v0r, r1r, wr)]
    wait_bytes(td3.at[pl.ds(0, N_DP - 1)], recv.at[4])
    four = total(jnp.sum(td3[...], axis=0))
    r1r1, r1w, v0w = four[0:1] + five[0], four[1:2] + five[1], four[2:3] + five[2]
    ww, waw, v0r1 = four[3:4] + five[3], (four[4:5] + five[4]) * step, four[5:6] + five[5]
    y0, y1, y2 = solve(m0, v0r1, v0w, r1r1, r1w, ww, waw)
    y0, y1, y2 = y0 * step, y1 * step, y2 * step
    sol_c = (y0 * v0c + y1 * r1c + y2 * wc) * (1.0 / root_rows)

    ys = [v * (1.0 / root_cols) for v in (y0, y1, y2)]
    sol_col = ys[0] * sol_cols[0] + ys[1] * sol_cols[1] + ys[2] * sol_cols[2]
    for t in range(tiles):
        at = pl.ds(t * LANES, LANES)
        g = gv[:, at].astype(F32)
        wv[:, at] = (kv[:, at] * (g - sol_col - lanes(sol_c, t)) * (1.0 / TEMP)).astype(BF16)
    ge = jnp.dot(wv[...], pv[...], preferred_element_type=F32)
    for j in range(4):
        rs_out[pl.ds(16 * j, 16)] = ge[:, j * LANES : (j + 1) * LANES].T.reshape(16, 8, LANES).astype(BF16)
    to_proto(lambda other: (rs_out.at[other], rs_in.at[pr]), 5)
    rs_in[pr] = rs_out[pr]
    wait_bytes(sx, recv.at[10])
    for c in range(cols // 512):
        at = pl.ds(c * 512, 512)
        both = sx[0, :, at].astype(F32) + sx[1, :, at].astype(F32)
        sf[:, at] = sp_own[x, :, at].astype(F32) + both

    scaled = []
    for d in range(N_DP):
        v0d = td2[d, 0:1, pl.ds(cols + LANES, LANES)]
        r1d = v0d - step * td2[d, 1:2, pl.ds(cols + LANES, LANES)]
        sol_d = (y0 * v0d + y1 * r1d + y2 * td3[d, 6:7, :]) * (1.0 / root_cols)
        scaled.append((eg[d, share, :] * sol_d).astype(BF16))
    lhs = jnp.concatenate(scaled, axis=1)
    for c in range(cols // 512):
        at = pl.ds(c * 512, 512)
        terms = jnp.dot(lhs, kf[:, at], preferred_element_type=F32)
        part = sf[:, at] - terms - uf[:, at] * (sol_c - guess)[:, c * 512 : (c + 1) * 512]
        op[:, at] = (part * (1.0 / TEMP)).astype(BF16)
    store = pltpu.make_async_copy(op, o_proto, in_sem.at[5])
    store.start()
    wait_bytes(rs_in.at[pl.ds(0, N_PROTO - 1)], recv.at[5])
    o_emb[...] = jnp.sum(rs_in[...].astype(F32), axis=0)

    store.wait()
    wait_bytes(hs.at[pl.ds(0, N_Z - 1)], send.at[11])
    wait_bytes(td1.at[pl.ds(0, N_DP - 1)], send.at[0])
    wait_bytes(tp1.at[pl.ds(0, N_PROTO - 1)], send.at[1])
    wait_bytes(td2.at[pl.ds(0, N_DP - 1)], send.at[2])
    wait_bytes(tp2.at[pl.ds(0, N_PROTO - 1)], send.at[3])
    wait_bytes(td3.at[pl.ds(0, N_DP - 1)], send.at[4])
    wait_bytes(rs_out.at[pl.ds(0, N_PROTO - 1)], send.at[5])
    wait_bytes(ef.at[pl.ds(0, 3 * LANES)], send.at[6])
    wait_bytes(ef.at[pl.ds(0, 4 * LANES)], send.at[7])
    wait_bytes(sp_out, send.at[8])
    wait_bytes(s2, send.at[9])
    wait_bytes(sx, send.at[10])


def shards(
    embeddings, prototypes, embedding_log_potential, prototype_log_potential, scaled_plan_gradient
):
    rows, width = embeddings.shape
    cols = prototypes.shape[0]
    share = width // N_DP
    any_space = pl.BlockSpec(memory_space=pl.ANY)
    vmem = pl.BlockSpec(memory_space=pltpu.VMEM)
    ge, gp = pl.pallas_call(
        functools.partial(body, rows * N_DP, cols * N_PROTO),
        out_shape=(
            jax.ShapeDtypeStruct((width // N_PROTO, rows), F32),
            jax.ShapeDtypeStruct((share, cols), BF16),
        ),
        in_specs=[any_space] * 5,
        out_specs=(vmem, any_space),
        scratch_shapes=[
            pltpu.VMEM((rows, width), BF16),
            pltpu.VMEM((N_DP, share, rows), BF16),
            pltpu.VMEM((cols, width), BF16),
            pltpu.VMEM((1, rows), F32),
            pltpu.VMEM((1, cols), F32),
            pltpu.VMEM((rows, cols), BF16),
            pltpu.VMEM((rows, cols), F32),
            pltpu.VMEM((rows, cols), BF16),
            pltpu.VMEM((N_DP, 2, cols + LANES), F32),
            pltpu.VMEM((N_DP, 2, cols + 2 * LANES), F32),
            pltpu.VMEM((N_DP, 8, LANES), F32),
            pltpu.VMEM((N_PROTO, 4, LANES), F32),
            pltpu.VMEM((N_PROTO, 4, LANES), F32),
            pltpu.VMEM((N_PROTO, 8, LANES), BF16),
            pltpu.VMEM((N_PROTO, 8, LANES), BF16),
            pltpu.VMEM((rows * N_DP, width), BF16),
            pltpu.VMEM((N_DP, LANES, rows), F32),
            pltpu.VMEM((rows * N_DP, LANES), F32),
            pltpu.VMEM((rows * N_DP, cols), BF16),
            pltpu.VMEM((share, cols), F32),
            pltpu.VMEM((share, cols), F32),
            pltpu.VMEM((4, share, cols), BF16),
            pltpu.VMEM((4, share, cols), BF16),
            pltpu.VMEM((4, share, cols), BF16),
            pltpu.VMEM((2, share // 2, cols), BF16),
            pltpu.VMEM((2, share, cols), BF16),
            pltpu.VMEM((share, cols), BF16),
            pltpu.VMEM((N_Z, 8, LANES), F32),
            pltpu.SemaphoreType.DMA((6,)),
            pltpu.SemaphoreType.DMA((12,)),
            pltpu.SemaphoreType.DMA((12,)),
        ],
        compiler_params=pltpu.CompilerParams(
            collective_id=0, has_side_effects=True, vmem_limit_bytes=56 * 1024 * 1024
        ),
    )(
        embeddings,
        prototypes,
        embedding_log_potential.reshape(1, rows),
        prototype_log_potential.reshape(1, cols),
        scaled_plan_gradient,
    )
    return ge.T, gp.T


def solution(mesh):
    return jax.shard_map(
        shards,
        mesh=mesh,
        in_specs=(P("dp", None), P("proto", None), P("dp"), P("proto"), P("dp", "proto")),
        out_specs=(P("dp", "proto"), P("proto", "dp")),
        check_vma=False,
    )
```

```python
import functools
import math

import jax
import jax.numpy as jnp
from jax import lax
from jax.experimental import pallas as pl
from jax.experimental.pallas import tpu as pltpu
from jax.sharding import PartitionSpec as P

MESH = pl.DeviceIdType.MESH
TEMP = 0.05
RIDGE = 0.05
N_DP = 8
N_Z = 8
N_Y = 8
N_PROTO = N_Z * N_Y
LANES = 128
F32 = jnp.float32
BF16 = jnp.bfloat16


def total(values):
    return jnp.sum(values, axis=1, keepdims=True)


def as_column(row):
    return jnp.broadcast_to(row, (LANES, LANES)).T


def as_row(acc):
    return jnp.sum(acc.T, axis=0, keepdims=True)


def hops(dz, dy):
    return min(dz, N_Z - dz) + min(dy, N_Y - dy)


FAR_FIRST = sorted(
    [(dz, dy) for dz in range(N_Z) for dy in range(N_Y) if dz or dy], key=lambda o: -hops(*o)
)
DP_FAR_FIRST = (4, 5, 3, 2, 6, 1, 7)
FAR = (4, 3, 5, 2, 6, 1, 7)


def wait_bytes(ref, sem):
    pltpu.make_async_copy(ref, ref, sem).wait()


def solve(m0, b1, b2, r1r1, r1w, ww, waw):
    g00, g01, g02 = m0, b1 - r1r1, b2 - r1w
    g11, g12, g22 = r1w + r1r1, ww + r1w, waw
    l10, l20 = g01 / g00, g02 / g00
    d1 = g11 - g01 * l10
    i1 = jnp.where(d1 > 1e-6 * g11, 1.0 / d1, 0.0)
    t = g12 - l20 * g01
    l21 = t * i1
    d2 = g22 - l20 * g02 - l21 * t
    i2 = jnp.where(d2 > 1e-6 * g22, 1.0 / d2, 0.0)
    z1 = b1 - l10 * m0
    z2 = b2 - l20 * m0 - l21 * z1
    y2 = z2 * i2
    y1 = z1 * i1 - l21 * y2
    y0 = 1.0 - l10 * y1 - l20 * y2
    return y0, y1, y2


def body(
    rows_all, cols_all,
    e_hbm, p_hbm, er_hbm, pc_hbm, g_hbm, o_emb, o_proto,
    ev, et, pv, er, pc, gv, kv, wv, td1, td2, td3, tp1, tp2, rs_out, rs_in,
    ef, eg, erc, kf, uf, sf, sp_out, sp_own, sp_in, s2, sx,
    op, in_sem, ready, send, recv,
):
    dp, pr = lax.axis_index("dp"), lax.axis_index("proto")
    z, y = lax.div(pr, N_Y), lax.rem(pr, N_Y)
    cols = pv.shape[0]
    tiles = cols // LANES
    root_cols = math.sqrt(cols_all)
    root_rows = math.sqrt(rows_all)
    coupling = 1.0 / (root_rows * root_cols)

    loads = [
        pltpu.make_async_copy(src, dst, in_sem.at[i])
        for i, (src, dst) in enumerate(
            [(e_hbm, ev), (p_hbm, pv), (er_hbm, er), (pc_hbm, pc), (g_hbm, gv)]
        )
    ]
    for load in loads:
        load.start()

    barrier = pltpu.get_barrier_semaphore()
    for k in FAR:
        pl.semaphore_signal(
            barrier, inc=1, device_id=(dp, z * N_Y + lax.rem(y + k, N_Y)), device_id_type=MESH
        )
        pl.semaphore_signal(
            barrier, inc=1, device_id=(dp, lax.rem(z + k, N_Z) * N_Y + y), device_id_type=MESH
        )
    for k in DP_FAR_FIRST:
        pl.semaphore_signal(
            barrier, inc=1, device_id=(lax.rem(dp + k, N_DP), pr), device_id_type=MESH
        )
    for load in loads:
        load.wait()

    def to_dp(buf, i):
        for k in DP_FAR_FIRST:
            pltpu.make_async_remote_copy(
                src_ref=buf.at[dp], dst_ref=buf.at[dp], send_sem=send.at[i], recv_sem=recv.at[i],
                device_id=(lax.rem(dp + k, N_DP), pr), device_id_type=MESH,
            ).start()

    def to_proto(make, i):
        for dz, dy in FAR_FIRST:
            other = lax.rem(z + dz, N_Z) * N_Y + lax.rem(y + dy, N_Y)
            src, dst = make(other)
            pltpu.make_async_remote_copy(
                src_ref=src, dst_ref=dst, send_sem=send.at[i], recv_sem=recv.at[i],
                device_id=(dp, other), device_id_type=MESH,
            ).start()

    er_col = as_column(er[...])
    row_acc = jnp.zeros((LANES, LANES), F32)
    rhs_acc = jnp.zeros((LANES, LANES), F32)
    wide = 256
    er_wide = jnp.concatenate([er_col, er_col], axis=1)
    for c in range(cols // wide):
        at = pl.ds(c * wide, wide)
        scores = lax.dot_general(
            ev[...], pv[at, :], (((1,), (1,)), ((), ())), preferred_element_type=F32
        )
        k = jnp.exp(scores * (1.0 / TEMP) + er_wide + pc[:, at])
        kv[:, at] = k
        w = gv[:, at].astype(F32) * k
        td1[dp, 0:1, at] = jnp.sum(k, axis=0, keepdims=True)
        td1[dp, 1:2, at] = jnp.sum(w, axis=0, keepdims=True)
        row_acc += k[:, :LANES] + k[:, LANES:]
        rhs_acc += w[:, :LANES] + w[:, LANES:]
    td1[dp, 0:1, pl.ds(cols, LANES)] = er[...]
    td1[dp, 1:2, pl.ds(cols, LANES)] = er[...]
    mine = pl.ds(pl.multiple_of(dp * LANES, LANES), LANES)

    pl.semaphore_wait(barrier, 21)
    to_dp(td1, 0)
    for k in FAR:
        pl.semaphore_signal(
            ready, inc=1, device_id=(dp, lax.rem(z + k, N_Z) * N_Y + y), device_id_type=MESH
        )
    row_part = as_row(row_acc)
    rhs_part = as_row(rhs_acc)

    for j in range(N_DP // 2):
        pair = ev[:, j * LANES : (j + 1) * LANES].astype(F32).T.astype(BF16)
        et[2 * j] = pair[:64]
        et[2 * j + 1] = pair[64:]
    wait_bytes(td1.at[pl.ds(0, N_DP - 1)], recv.at[0])
    col_pair = jnp.sum(td1[:, :, pl.ds(0, cols)], axis=0)
    dc = col_pair[0:1] * (1.0 / rows_all) + RIDGE
    v0c = col_pair[1:2] * (1.0 / root_rows)

    def lanes(row, t):
        return row[:, t * LANES : (t + 1) * LANES]

    def fold(row):
        return functools.reduce(lambda a, b: a + b, [lanes(row, t) for t in range(tiles)])

    def k_times(*vectors):
        accs = [jnp.zeros((LANES, LANES), F32) for _ in vectors]
        for t in range(tiles):
            k = kv[:, t * LANES : (t + 1) * LANES]
            accs = [a + k * lanes(v, t) for a, v in zip(accs, vectors)]
        return [as_row(a) for a in accs]

    (kv0,) = k_times(v0c)
    lane = lax.broadcasted_iota(jnp.int32, (1, LANES), 1)

    def by_two(row):
        return row + pltpu.roll(row, 64, 1)

    def by_four(row):
        row = by_two(row)
        return row + pltpu.roll(row, 32, 1)

    tp1[pr] = jnp.concatenate(
        [row_part, rhs_part, kv0,
         jnp.where(lane < 64, by_two(fold(v0c * v0c)), by_two(fold(v0c * dc * v0c)))],
        axis=0,
    )
    pl.semaphore_wait(ready, 7)
    to_proto(lambda other: (tp1.at[pr], tp1.at[pr]), 1)

    x, core = lax.div(dp, 2), lax.rem(dp, 2)
    sibling = 2 * x + 1 - core

    def block(d):
        return ef.at[pl.ds(pl.multiple_of(d * LANES, LANES), LANES)]

    for k in (2, 1, 3):
        pltpu.make_async_remote_copy(
            src_ref=ev, dst_ref=block(dp), send_sem=send.at[6], recv_sem=recv.at[6],
            device_id=(2 * lax.rem(x + k, 4) + core, pr), device_id_type=MESH,
        ).start()
    ef[mine, :] = ev[...]

    guess = col_pair[1:2] * (1.0 / rows_all) / dc
    for t in range(tiles):
        at = pl.ds(t * LANES, LANES)
        wv[:, at] = (kv[:, at] * (gv[:, at].astype(F32) - lanes(guess, t))).astype(BF16)

    def weighted_terms(to, first):
        lhs = jnp.concatenate([et[2 * j + first] for j in range(4)], axis=0)
        for c in range(cols // 512):
            at = pl.ds(c * 512, 512)
            part = jnp.dot(lhs, wv[:, at], preferred_element_type=F32).astype(BF16)
            for j in range(4):
                to[j, :, at] = part[64 * j : 64 * j + 64]

    weighted_terms(sp_out, 1 - core)
    pltpu.make_async_remote_copy(
        src_ref=sp_out, dst_ref=sp_in, send_sem=send.at[8], recv_sem=recv.at[8],
        device_id=(sibling, pr), device_id_type=MESH,
    ).start()
    weighted_terms(sp_own, core)
    for d in range(N_DP):
        erc[d * LANES : (d + 1) * LANES, :] = as_column(td1[d, 0:1, cols:])
    wait_bytes(tp1.at[pl.ds(0, N_PROTO - 1)], recv.at[1])
    one = jnp.sum(tp1[...], axis=0)
    dr = one[0:1] * (1.0 / cols_all) + RIDGE
    v0r = one[1:2] * (1.0 / root_cols)
    kv0 = one[2:3]
    s0 = total(jnp.where(lane < 64, one[3:4], 0.0))
    s1 = total(jnp.where(lane < 64, 0.0, one[3:4]))
    p_r = dr * v0r + coupling * kv0

    v0_col, p_col = as_column(v0r), as_column(p_r)
    for t in range(tiles):
        at = pl.ds(t * LANES, LANES)
        k = kv[:, at]
        td2[dp, 0:1, at] = jnp.sum(k * v0_col, axis=0, keepdims=True)
        td2[dp, 1:2, at] = jnp.sum(k * p_col, axis=0, keepdims=True)
    td2[dp, 0:1, pl.ds(cols, LANES)] = v0r * v0r
    td2[dp, 1:2, pl.ds(cols, LANES)] = v0r * (dr * v0r + (2.0 * coupling) * kv0)
    td2[dp, 0:1, pl.ds(cols + LANES, LANES)] = v0r
    td2[dp, 1:2, pl.ds(cols + LANES, LANES)] = p_r
    to_dp(td2, 2)

    def whole_kernel(c):
        at = pl.ds(c * wide, wide)
        scores = lax.dot_general(
            ef[...], pv[at, :], (((1,), (1,)), ((), ())), preferred_element_type=F32
        )
        shift = jnp.concatenate([erc[...], erc[...]], axis=1)
        kf[:, at] = jnp.exp(scores * (1.0 / TEMP) + shift + pc[:, at]).astype(BF16)

    wait_bytes(ef.at[pl.ds(0, 3 * LANES)], recv.at[6])
    for j in range(4):
        pltpu.make_async_remote_copy(
            src_ref=block(2 * j + core), dst_ref=block(2 * j + core),
            send_sem=send.at[7], recv_sem=recv.at[7],
            device_id=(sibling, pr), device_id_type=MESH,
        ).start()
    wait_bytes(sp_in, recv.at[8])
    for j in range(4):
        sp_own[j] = (sp_own[j].astype(F32) + sp_in[j].astype(F32)).astype(BF16)
    wait_bytes(td2.at[pl.ds(0, N_DP - 1)], recv.at[2])
    two = jnp.sum(td2[...], axis=0)
    m0 = s0 + total(two[0:1, cols : cols + LANES])
    m1 = s1 + total(two[1:2, cols : cols + LANES])
    theta = m1 / m0
    step = m0 / m1
    ktv0, ktp = two[0:1, :cols], two[1:2, :cols]
    r1r = v0r - step * p_r
    r1c = v0c - step * (dc * v0c + coupling * ktv0)
    ktr1 = ktv0 - step * ktp
    wc = step * (dc * r1c + coupling * ktr1) - r1c

    kr1, kw = k_times(r1c, wc)
    q = [by_four(fold(v)) for v in
         (r1c * r1c, r1c * wc, v0c * wc, wc * wc, wc * dc * wc, v0c * r1c)]
    tp2[pr] = jnp.concatenate(
        [kr1, kw,
         jnp.where(lane < 64, jnp.where(lane < 32, q[0], q[1]), jnp.where(lane < 96, q[2], q[3])),
         jnp.where(lane < 64, jnp.where(lane < 32, q[4], q[5]), 0.0)],
        axis=0,
    )
    to_proto(lambda other: (tp2.at[pr], tp2.at[pr]), 3)
    right, left, across = (lax.rem(x + k, 4) for k in (1, 3, 2))
    for i, to in enumerate((right, left)):
        pltpu.make_async_remote_copy(
            src_ref=sp_own.at[across, pl.ds(32 * i, 32)], dst_ref=s2.at[i],
            send_sem=send.at[9], recv_sem=recv.at[9],
            device_id=(2 * to + core, pr), device_id_type=MESH,
        ).start()
    wait_bytes(ef.at[pl.ds(0, 4 * LANES)], recv.at[7])
    for d in range(N_DP):
        eg[d] = ef[d * LANES : (d + 1) * LANES, pl.ds(pl.multiple_of(x * LANES, LANES), LANES)].astype(F32).T
    for c in range(cols // wide):
        whole_kernel(c)
    share = pl.ds(pl.multiple_of(64 * core, 64), 64)
    lhs = jnp.concatenate([eg[d, share, :] for d in range(N_DP)], axis=1).astype(BF16)
    for c in range(cols // 512):
        at = pl.ds(c * 512, 512)
        uf[:, at] = jnp.dot(lhs, kf[:, at], preferred_element_type=F32)
    wait_bytes(tp2.at[pl.ds(0, N_PROTO - 1)], recv.at[3])
    three = jnp.sum(tp2[...], axis=0)
    kr1, kw = three[0:1], three[1:2]
    wr = step * (dr * r1r + coupling * kr1) - r1r
    td3[dp] = jnp.concatenate(
        [r1r * r1r, r1r * wr, v0r * wr, wr * wr, wr * (dr * wr + (2.0 * coupling) * kw), v0r * r1r,
         wr, jnp.zeros((1, LANES), F32)],
        axis=0,
    )
    to_dp(td3, 4)
    wait_bytes(s2, recv.at[9])
    for i, to in enumerate((right, left)):
        half = pl.ds(32 * i, 32)
        sp_own[to, half] = (sp_own[to, half].astype(F32) + s2[i].astype(F32)).astype(BF16)
        pltpu.make_async_remote_copy(
            src_ref=sp_own.at[to], dst_ref=sx.at[i], send_sem=send.at[10], recv_sem=recv.at[10],
            device_id=(2 * to + core, pr), device_id_type=MESH,
        ).start()
    five = [
        total(jnp.where((lane >= 32 * g) & (lane < 32 * g + 32), three[r : r + 1], 0.0))
        for r, g in ((2, 0), (2, 1), (2, 2), (2, 3), (3, 0), (3, 1))
    ]
    sol_cols = [as_column(v) for v in (v0r, r1r, wr)]
    wait_bytes(td3.at[pl.ds(0, N_DP - 1)], recv.at[4])
    four = total(jnp.sum(td3[...], axis=0))
    r1r1, r1w, v0w = four[0:1] + five[0], four[1:2] + five[1], four[2:3] + five[2]
    ww, waw, v0r1 = four[3:4] + five[3], (four[4:5] + five[4]) * step, four[5:6] + five[5]
    y0, y1, y2 = solve(m0, v0r1, v0w, r1r1, r1w, ww, waw)
    y0, y1, y2 = y0 * step, y1 * step, y2 * step
    sol_c = (y0 * v0c + y1 * r1c + y2 * wc) * (1.0 / root_rows)

    ys = [v * (1.0 / root_cols) for v in (y0, y1, y2)]
    sol_col = ys[0] * sol_cols[0] + ys[1] * sol_cols[1] + ys[2] * sol_cols[2]
    for t in range(tiles):
        at = pl.ds(t * LANES, LANES)
        g = gv[:, at].astype(F32)
        wv[:, at] = (kv[:, at] * (g - sol_col - lanes(sol_c, t)) * (1.0 / TEMP)).astype(BF16)
    ge = jnp.dot(wv[...], pv[...], preferred_element_type=F32)
    for j in range(4):
        rs_out[pl.ds(16 * j, 16)] = ge[:, j * LANES : (j + 1) * LANES].T.reshape(16, 8, LANES).astype(BF16)
    to_proto(lambda other: (rs_out.at[other], rs_in.at[pr]), 5)
    rs_in[pr] = rs_out[pr]
    wait_bytes(sx, recv.at[10])
    for c in range(cols // 512):
        at = pl.ds(c * 512, 512)
        both = sx[0, :, at].astype(F32) + sx[1, :, at].astype(F32)
        sf[:, at] = sp_own[x, :, at].astype(F32) + both

    scaled = []
    for d in range(N_DP):
        v0d = td2[d, 0:1, pl.ds(cols + LANES, LANES)]
        r1d = v0d - step * td2[d, 1:2, pl.ds(cols + LANES, LANES)]
        sol_d = (y0 * v0d + y1 * r1d + y2 * td3[d, 6:7, :]) * (1.0 / root_cols)
        scaled.append((eg[d, share, :] * sol_d).astype(BF16))
    lhs = jnp.concatenate(scaled, axis=1)
    for c in range(cols // 512):
        at = pl.ds(c * 512, 512)
        terms = jnp.dot(lhs, kf[:, at], preferred_element_type=F32)
        part = sf[:, at] - terms - uf[:, at] * (sol_c - guess)[:, c * 512 : (c + 1) * 512]
        op[:, at] = (part * (1.0 / TEMP)).astype(BF16)
    store = pltpu.make_async_copy(op, o_proto, in_sem.at[5])
    store.start()
    wait_bytes(rs_in.at[pl.ds(0, N_PROTO - 1)], recv.at[5])
    o_emb[...] = jnp.sum(rs_in[...].astype(F32), axis=0)

    store.wait()
    wait_bytes(td1.at[pl.ds(0, N_DP - 1)], send.at[0])
    wait_bytes(tp1.at[pl.ds(0, N_PROTO - 1)], send.at[1])
    wait_bytes(td2.at[pl.ds(0, N_DP - 1)], send.at[2])
    wait_bytes(tp2.at[pl.ds(0, N_PROTO - 1)], send.at[3])
    wait_bytes(td3.at[pl.ds(0, N_DP - 1)], send.at[4])
    wait_bytes(rs_out.at[pl.ds(0, N_PROTO - 1)], send.at[5])
    wait_bytes(ef.at[pl.ds(0, 3 * LANES)], send.at[6])
    wait_bytes(ef.at[pl.ds(0, 4 * LANES)], send.at[7])
    wait_bytes(sp_out, send.at[8])
    wait_bytes(s2, send.at[9])
    wait_bytes(sx, send.at[10])


def shards(
    embeddings, prototypes, embedding_log_potential, prototype_log_potential, scaled_plan_gradient
):
    rows, width = embeddings.shape
    cols = prototypes.shape[0]
    share = width // N_DP
    any_space = pl.BlockSpec(memory_space=pl.ANY)
    vmem = pl.BlockSpec(memory_space=pltpu.VMEM)
    ge, gp = pl.pallas_call(
        functools.partial(body, rows * N_DP, cols * N_PROTO),
        out_shape=(
            jax.ShapeDtypeStruct((width // N_PROTO, rows), F32),
            jax.ShapeDtypeStruct((share, cols), BF16),
        ),
        in_specs=[any_space] * 5,
        out_specs=(vmem, any_space),
        scratch_shapes=[
            pltpu.VMEM((rows, width), BF16),
            pltpu.VMEM((N_DP, share, rows), BF16),
            pltpu.VMEM((cols, width), BF16),
            pltpu.VMEM((1, rows), F32),
            pltpu.VMEM((1, cols), F32),
            pltpu.VMEM((rows, cols), BF16),
            pltpu.VMEM((rows, cols), F32),
            pltpu.VMEM((rows, cols), BF16),
            pltpu.VMEM((N_DP, 2, cols + LANES), F32),
            pltpu.VMEM((N_DP, 2, cols + 2 * LANES), F32),
            pltpu.VMEM((N_DP, 8, LANES), F32),
            pltpu.VMEM((N_PROTO, 4, LANES), F32),
            pltpu.VMEM((N_PROTO, 4, LANES), F32),
            pltpu.VMEM((N_PROTO, 8, LANES), BF16),
            pltpu.VMEM((N_PROTO, 8, LANES), BF16),
            pltpu.VMEM((rows * N_DP, width), BF16),
            pltpu.VMEM((N_DP, LANES, rows), F32),
            pltpu.VMEM((rows * N_DP, LANES), F32),
            pltpu.VMEM((rows * N_DP, cols), BF16),
            pltpu.VMEM((share, cols), F32),
            pltpu.VMEM((share, cols), F32),
            pltpu.VMEM((4, share, cols), BF16),
            pltpu.VMEM((4, share, cols), BF16),
            pltpu.VMEM((4, share, cols), BF16),
            pltpu.VMEM((2, share // 2, cols), BF16),
            pltpu.VMEM((2, share, cols), BF16),
            pltpu.VMEM((share, cols), BF16),
            pltpu.SemaphoreType.DMA((6,)),
            pltpu.SemaphoreType.REGULAR,
            pltpu.SemaphoreType.DMA((11,)),
            pltpu.SemaphoreType.DMA((11,)),
        ],
        compiler_params=pltpu.CompilerParams(
            collective_id=0, has_side_effects=True, vmem_limit_bytes=56 * 1024 * 1024
        ),
    )(
        embeddings,
        prototypes,
        embedding_log_potential.reshape(1, rows),
        prototype_log_potential.reshape(1, cols),
        scaled_plan_gradient,
    )
    return ge.T, gp.T


def solution(mesh):
    return jax.shard_map(
        shards,
        mesh=mesh,
        in_specs=(P("dp", None), P("proto", None), P("dp"), P("proto"), P("dp", "proto")),
        out_specs=(P("dp", "proto"), P("proto", "dp")),
        check_vma=False,
    )
```
